128 devices in a mesh: dp: 8 (over z, core), vocab: 16 (over y, x).
Axes of the slice: x: 4, y: 4, z: 4, core: 2. Of those that a mesh axis runs over, the one named last changes fastest.
Arguments:
- hidden: bfloat16 [2048, 4096], P(('dp', 'vocab')), may hold values from -64 to 64
- head_weight: bfloat16 [4096, 128256], P(None, ('dp', 'vocab')), may hold values from -0.0625 to 0.0625
- targets: int32 [2048], P(('dp', 'vocab')), may hold values from 0 to 128255
- bench_ids: int32 [2048], P(('dp', 'vocab')), may hold values from 0 to 39, as said below
- valid: int32 [2048], P(('dp', 'vocab')), may hold values from 0 to 1, as said below
- seq_lengths: int32 [64], replicated, may hold values from 1 to 64, 2048 in all
Outputs:
- token_loss: float32 [2048], P(('dp', 'vocab'))
- bench_loss: float32 [40], replicated
- bench_count: float32 [40], replicated
The draws below stay inside these ranges and needn't reach their ends.
Inputs may be any that keep to these rules, and one draw needn't show every extreme that they name: `valid`: among the 16 positions of one device (aligned blocks) at most 8 have validity 1, and some block has exactly 8. `bench_ids`: A benchmark may have no positions in the window.
All inputs are finite; a program needn't handle non-finite values.
Results may differ from the reference program's by a relative error of at most 0.0003.
Values may be sent and summed in bfloat16 or wider, within the bound.
No kernel may reach another device: no remote copies, remote signals or barrier semaphores. Data moves between devices by JAX's collectives and lax.ppermute only.
A program may use at most 64 MiB of HBM per device.

```python
import math
import jax
import jax.numpy as jnp
import numpy as np
from jax import lax

D = 4096
VOCAB = 128256
BENCH = 40
TOK_DEV = 16
TOKENS = 2048
SEQS = 64
MAXLEN = 64


def head_column(key, column_id):
    column_key = jax.random.fold_in(jax.random.fold_in(key, 4242), column_id)
    values = jnp.clip(jax.random.normal(column_key, (D,), jnp.float32), -4.0, 4.0) * D ** (-0.5)
    return values.astype(jnp.bfloat16).astype(jnp.float32)


def draw_head_weight(key, part):
    columns = jax.vmap(head_column, in_axes=(None, 0))(key, jnp.arange(VOCAB, dtype=jnp.int32))
    return columns.T.astype(jnp.bfloat16)


def draw_hidden(key, part):
    normal_part = jax.random.normal(jax.random.fold_in(key, 17), (TOKENS, D), jnp.float32)
    values = 3.0 * jnp.clip(normal_part, -5.0, 5.0)
    return values.astype(jnp.bfloat16)


def draw_bench_ids(key, part):
    order = jax.random.permutation(jax.random.fold_in(key, 51), BENCH).astype(jnp.int32)
    first_rank = jax.random.randint(jax.random.fold_in(key, 52), (TOKENS,), 0, BENCH - 1)
    second_rank = jax.random.randint(jax.random.fold_in(key, 53), (TOKENS,), 0, BENCH - 1)
    ranks = jnp.minimum(first_rank, second_rank)
    return order[ranks].astype(jnp.int32)


def permuted(key_item):
    return jax.random.permutation(key_item, TOK_DEV)


def draw_valid(key, part):
    device_count = TOKENS // TOK_DEV
    capacity = TOK_DEV // 2
    fewest = max(capacity // 3, 1)
    per_device = jax.random.randint(jax.random.fold_in(key, 31), (device_count,), fewest, capacity + 1)
    busiest = jax.random.randint(jax.random.fold_in(key, 32), (), 0, device_count)
    bottom = (busiest + 1 + jax.random.randint(jax.random.fold_in(key, 33), (), 0, device_count - 1)) % device_count
    per_device = per_device.at[busiest].set(capacity).at[bottom].set(fewest)
    rank_table = jax.vmap(permuted)(jax.random.split(jax.random.fold_in(key, 34), device_count))
    return (rank_table < per_device[:, None]).astype(jnp.int32).reshape(TOKENS)


def plant(drawn, own_key, least, high):
    dims = drawn.shape
    index_at = [jax.random.randint(jax.random.fold_in(own_key, axis), (), 0, dims[axis]) for axis in range(len(dims))]
    drawn = drawn.at[tuple(index_at)].set(least)
    longest = dims.index(max(dims))
    index_at[longest] = (index_at[longest] + 1) % dims[longest]
    return drawn.at[tuple(index_at)].set(high)


def wide_ids(own_key, dims, amount, skew):
    weights = [min(1 << octave, amount + 1 - (1 << octave)) * (1 << 20) // math.isqrt((1 << octave) ** skew) + 1 for octave in range((amount + 1).bit_length()) if 1 << octave <= amount]
    scale = 1 + sum(weights) // (1 << 30)
    listing = np.cumsum(np.array([max(1, weight // scale) for weight in weights]))
    ticket = jax.random.randint(jax.random.fold_in(own_key, 1), dims, 0, int(listing[len(weights) - 1]))
    start = jnp.left_shift(1, jnp.searchsorted(jnp.asarray(listing, jnp.int32), ticket, side="right").astype(jnp.int32))
    rank = start - 1 + jax.random.randint(jax.random.fold_in(own_key, 4), dims, 0, 1 << 30) % jnp.minimum(start, amount + 1 - start)
    return jax.random.permutation(jax.random.fold_in(own_key, 2), amount)[rank].astype(jnp.int32)


def length_profile(count, total, limit, skew):
    portions = [(1 << 20) // math.isqrt(standing ** skew) + 1 for standing in range(2, count + 1)]
    rest, counts = total - limit - (count - 1), [1] * (count - 1)
    while rest > 0:
        candidates = [i for i in range(count - 1) if counts[i] < limit]
        whole, left = sum([portions[i] for i in candidates]), rest
        for i in candidates:
            addition = min(limit - counts[i], max(1, left * portions[i] // whole), rest)
            counts[i] = counts[i] + addition
            rest = rest - addition
    return np.array([limit] + counts)


def ragged(key, amount, total, bound, lean):
    if amount == 2:
        one = jax.random.randint(key, (), max(1, total - bound), min(bound, total - 1) + 1)
        return jnp.stack([one, total - one])
    sizes = jnp.asarray(length_profile(amount, total, bound, lean), jnp.int32)
    pairs = (amount - 1) // 2
    source_of, sink = sizes[1:1 + 2 * pairs:2], sizes[2:2 + 2 * pairs:2]
    slack = jnp.minimum(source_of - 1, bound - sink)
    passed = jax.random.randint(jax.random.fold_in(key, 1), (pairs,), 0, 1 << 20) % (slack + 1)
    sizes = sizes.at[1:1 + 2 * pairs:2].set(source_of - passed).at[2:2 + 2 * pairs:2].set(sink + passed)
    return sizes[jax.random.permutation(jax.random.fold_in(key, 2), amount)]


def setup_inputs(seed: int = 0) -> dict:
    streams_of = jax.random.split(jax.random.key(seed), 7)
    return {
        "hidden": draw_hidden(jax.random.fold_in(streams_of[6], 71), 0),
        "head_weight": draw_head_weight(jax.random.fold_in(streams_of[6], 71), 0),
        "targets": plant(wide_ids(streams_of[2], (TOKENS,), VOCAB, 2), jax.random.fold_in(streams_of[2], 3), 0, VOCAB - 1).astype(jnp.int32),
        "bench_ids": draw_bench_ids(jax.random.fold_in(streams_of[6], 71), 0),
        "valid": draw_valid(jax.random.fold_in(streams_of[6], 71), 0),
        "seq_lengths": ragged(streams_of[5], SEQS, TOKENS, MAXLEN, 2).astype(jnp.int32),
    }


def reference(hidden, head_weight, targets, bench_ids, valid, seq_lengths):
    seq_ends = (jnp.cumsum(seq_lengths) - 1).astype(jnp.int32)
    positions = jnp.arange(TOKENS, dtype=jnp.int32)
    is_end = jnp.any(positions[:, None] == seq_ends[None, :], axis=1)
    scored = valid * (1 - is_end.astype(jnp.int32))

    def score_block(inputs):
        row_block, target_ids = inputs
        logits = jnp.dot(row_block, head_weight, preferred_element_type=jnp.float32)
        row_top = jnp.max(logits, axis=1)
        row_total = jnp.sum(jnp.exp(logits - row_top[:, None]), axis=1)
        target_logit = jnp.take_along_axis(logits, target_ids[:, None], axis=1)[:, 0]
        return row_top + jnp.log(row_total) - target_logit

    losses = lax.map(score_block, (hidden.reshape(TOKENS // TOK_DEV, TOK_DEV, D), targets.reshape(TOKENS // TOK_DEV, TOK_DEV)))
    scored_float = scored.astype(jnp.float32)
    token_loss = losses.reshape(TOKENS) * scored_float
    onehot = (bench_ids[:, None] == jnp.arange(BENCH, dtype=jnp.int32)[None, :]).astype(jnp.float32)
    loss_sums = jnp.sum(onehot * token_loss[:, None], axis=0)
    token_counts = jnp.sum(onehot * scored_float[:, None], axis=0)
    bench_loss = loss_sums / jnp.maximum(token_counts, 1.0)
    return (token_loss, bench_loss, token_counts)
```

```python
import jax
import jax.numpy as jnp
from jax import lax
from jax.experimental import pallas as pl
from jax.experimental.pallas import tpu as pltpu
from jax.sharding import Mesh
from jax.sharding import PartitionSpec as P

BENCH = 40
N_DEV = 128
LAB = 128
ROWS = (24, 24, 16)
STARTS = (0, 24, 48)
HALF_STARTS = (0, 96, 192)
F32 = jnp.float32


def coords(d):
    return (d // 32, (d // 4) % 4, d % 4), (d // 16) % 2


def flipped(d, axis, bit):
    (z, y, x), core = coords(d)
    p = [z, y, x]
    p[axis] = 3 - p[axis] if bit else p[axis] ^ 1
    return ((p[0] * 2 + core) * 4 + p[1]) * 4 + p[2]


def exchange(v, axis, bits):
    pairs = [(d, flipped(d, axis, bits[coords(d)[1]])) for d in range(N_DEV)]
    return lax.ppermute(v, "d", pairs)


def core_swap(v):
    return lax.ppermute(v, "d", [(d, d ^ 16) for d in range(N_DEV)])


def cube_bits(p):
    return (p ^ (p >> 1)) & 1, p >> 1


def score_kernel(offset_ref, x_ref, w_ref, out_ref, acc_ref):
    depth = w_ref.shape[1]
    rows = x_ref.shape[0]
    r = lax.broadcasted_iota(jnp.int32, (8, LAB), 0)
    c = lax.broadcasted_iota(jnp.int32, (8, LAB), 1)
    digit = jnp.where(c == 0, 65536.0, jnp.where(c == 1, 256.0, 1.0))
    sel = jnp.where((r == 5) & (c < 3), digit, jnp.where(((r == 3) | (r == 4)) & (r == c), 1.0, 0.0))
    dims = (((1,), (1,)), ((), ()))
    labels = lax.dot_general(
        sel.astype(jnp.bfloat16), x_ref[:, depth:], dims, preferred_element_type=F32
    )
    acc_ref[...] = lax.dot_general(w_ref[...], x_ref[:, :depth], dims, preferred_element_type=F32)
    logits = acc_ref[...]
    top = jnp.max(logits, axis=0, keepdims=True)
    total = jnp.sum(jnp.exp(logits - top), axis=0, keepdims=True)
    local = labels[5:6].astype(jnp.int32) - offset_ref[0]
    hit = lax.broadcasted_iota(jnp.int32, logits.shape, 0) == local
    target = jnp.sum(jnp.where(hit, logits, 0.0), axis=0, keepdims=True)
    k = lax.broadcasted_iota(jnp.int32, (8, rows), 0)
    out_ref[...] = jnp.where(k == 0, top, jnp.where(k == 1, total, jnp.where(k == 2, target, labels)))


def score(offset, x, w):
    rows = x.shape[0]
    vocab, depth = w.shape
    return pl.pallas_call(
        score_kernel,
        out_shape=jax.ShapeDtypeStruct((8, rows), F32),
        in_specs=[
            pl.BlockSpec(memory_space=pltpu.SMEM),
            pl.BlockSpec(memory_space=pltpu.VMEM),
            pl.BlockSpec(memory_space=pltpu.VMEM),
        ],
        out_specs=pl.BlockSpec(memory_space=pltpu.VMEM),
        scratch_shapes=[pltpu.VMEM((vocab, rows), F32)],
        compiler_params=pltpu.CompilerParams(vmem_limit_bytes=40 << 20),
        cost_estimate=pl.CostEstimate(
            flops=2 * rows * vocab * depth, bytes_accessed=2 * vocab * depth, transcendentals=rows * vocab
        ),
        name="score",
    )(offset, x, w)


def place_kernel(where_ref, own1, sib1, own2, sib2, stats_ref, labels_ref, all_ref):
    first = where_ref[0] == 0
    for half, (own, sib) in enumerate(((own1, sib1), (own2, sib2))):
        a, b = own[...], sib[...]
        by_core = (jnp.where(first, a, b), jnp.where(first, b, a))
        for g in range(3):
            for i in range(4):
                r = 4 * half + i
                rel = sum(((r >> k) & 1) << ((g + k) % 3) for k in range(3))
                at = HALF_STARTS[g] + i * ROWS[g]
                for core in range(2):
                    row = where_ref[1 + core] ^ rel
                    to = core * 64 + STARTS[g]
                    all_ref[row, :, to : to + ROWS[g]] = by_core[core][:, at : at + ROWS[g]]
    for kind in range(3):
        stats_ref[kind] = all_ref[:, kind, :]
    for kind in range(2):
        labels_ref[kind] = all_ref[:, 3 + kind, :]


def place(where, *parts):
    return pl.pallas_call(
        place_kernel,
        out_shape=(jax.ShapeDtypeStruct((3, 8, 128), F32), jax.ShapeDtypeStruct((2, 8, 128), F32)),
        in_specs=[pl.BlockSpec(memory_space=pltpu.SMEM)] + [pl.BlockSpec(memory_space=pltpu.VMEM)] * 4,
        out_specs=(pl.BlockSpec(memory_space=pltpu.VMEM),) * 2,
        scratch_shapes=[pltpu.VMEM((8, 8, 128), F32)],
        name="place",
    )(where, *parts)


def merged(a, b):
    best = jnp.maximum(a[0], b[0])
    total = a[1] * jnp.exp(a[0] - best) + b[1] * jnp.exp(b[0] - best)
    return jnp.stack([best, total, a[2] + b[2]])


def body(hidden, head_weight, targets, bench_ids, valid, seq_lengths):
    rows, depth = hidden.shape
    vocab = head_weight.shape[1]
    me = lax.axis_index("d")
    place_of, core = coords(me)
    bits = [cube_bits(p) for p in place_of]
    is_first = core == 0
    early = [jnp.where(is_first, b[1], b[0]) for b in bits]

    seqs = jnp.arange(seq_lengths.shape[0])
    seq_ends = jnp.sum(jnp.where(seqs[None, :] <= seqs[:, None], seq_lengths[None, :], 0), axis=1) - 1
    token = jnp.arange(rows, dtype=jnp.int32)
    is_end = jnp.any(seq_ends[:, None] == (me * rows + token)[None, :], axis=0)
    scored = valid * (1 - is_end.astype(jnp.int32))
    kept = rows // 2
    upto = token[None, :] <= token[:, None]
    valid_rank = jnp.sum(jnp.where(upto, valid[None, :], 0), axis=1) - 1
    slot = jnp.where(valid == 1, valid_rank, jnp.sum(valid) + token - valid_rank - 1)
    selector = jnp.arange(kept, dtype=jnp.int32)[:, None] == slot[None, :]
    column = jnp.arange(LAB)[None, :]
    labels = jnp.where(column == 0, (targets >> 16)[:, None], 0)
    labels = jnp.where(column == 1, ((targets >> 8) & 255)[:, None], labels)
    labels = jnp.where(column == 2, (targets & 255)[:, None], labels)
    labels = jnp.where(column == 3, bench_ids[:, None], labels)
    labels = jnp.where(column == 4, scored[:, None], labels)
    wide = jnp.concatenate([hidden, labels.astype(jnp.bfloat16)], axis=1)
    x = jnp.dot(selector.astype(jnp.bfloat16), wide, preferred_element_type=F32).astype(jnp.bfloat16)

    for axis in range(3):
        got = exchange(x, axis, (1, 0))
        x = jnp.where(
            early[axis] == 0, jnp.concatenate([x, got], 0), jnp.concatenate([got, x], 0)
        )
    held = [x[s : s + n] for s, n in zip(STARTS, ROWS)]
    for k in range(2):
        got = [exchange(held[g], (g + k) % 3, (0, 1)) for g in range(3)]
        held = [jnp.concatenate([a, b], 0) for a, b in zip(held, got)]
    w = head_weight.T
    offset = (me * vocab).reshape(1)
    last = [exchange(held[g], (g + 2) % 3, (0, 1)) for g in range(3)]
    own1 = jnp.concatenate(held, 0)
    sib1 = core_swap(own1)
    own2 = jnp.concatenate(last, 0)
    sib2 = core_swap(own2)
    parts = [score(offset, v, w) for v in (own1, sib1, own2, sib2)]
    by_core = [sum(b[k] << axis for axis, b in enumerate(bits)) for k in range(2)]
    stats, label_rows = place(jnp.stack([core, *by_core]), *parts)
    stats = merged(stats, core_swap(stats))
    for axis in range(3):
        for bit in range(2):
            stats = merged(stats, exchange(stats, axis, (bit, bit)))
    losses = stats[0] + jnp.log(stats[1]) - stats[2]
    bench_all, scored_all = label_rows[0], label_rows[1]
    me_early = early[0] + 2 * early[1] + 4 * early[2]
    own_at = jnp.where(is_first, *by_core) * 128 + core * 64 + me_early * kept
    own = lax.dynamic_slice_in_dim(losses.reshape(-1), own_at, kept)
    spread = jnp.sum(jnp.where(selector, own[:, None], 0.0), axis=0)
    token_loss = spread * scored.astype(F32)
    onehot = bench_all.reshape(-1)[:, None] == jnp.arange(BENCH, dtype=F32)[None, :]
    loss_sums = jnp.sum(jnp.where(onehot, (losses * scored_all).reshape(-1)[:, None], 0.0), axis=0)
    counts = jnp.sum(jnp.where(onehot, scored_all.reshape(-1)[:, None], 0.0), axis=0)
    return token_loss, loss_sums / jnp.maximum(counts, 1.0), counts


def solution(mesh):
    flat = Mesh(mesh.devices.reshape(-1), ("d",))
    in_specs = (P("d", None), P(None, "d"), P("d"), P("d"), P("d"), P())
    return jax.shard_map(
        body, mesh=flat, in_specs=in_specs, out_specs=(P("d"), P(), P()), check_vma=False
    )
```

```python
import jax
import jax.numpy as jnp
from jax import lax
from jax.experimental import pallas as pl
from jax.experimental.pallas import tpu as pltpu
from jax.sharding import Mesh
from jax.sharding import PartitionSpec as P

BENCH = 40
N_DEV = 128
LAB = 128
ROWS = (24, 24, 16)
STARTS = (0, 24, 48)
HALF_STARTS = (0, 96, 192)
F32 = jnp.float32
CHUNK = 256
LIMIT = 12 << 20


def coords(d):
    return (d // 32, (d // 4) % 4, d % 4), (d // 16) % 2


def flipped(d, axis, bit):
    (z, y, x), core = coords(d)
    p = [z, y, x]
    p[axis] = 3 - p[axis] if bit else p[axis] ^ 1
    return ((p[0] * 2 + core) * 4 + p[1]) * 4 + p[2]


def exchange(v, axis, bits):
    pairs = [(d, flipped(d, axis, bits[coords(d)[1]])) for d in range(N_DEV)]
    return lax.ppermute(v, "d", pairs)


def core_swap(v):
    return lax.ppermute(v, "d", [(d, d ^ 16) for d in range(N_DEV)])


def cube_bits(p):
    return (p ^ (p >> 1)) & 1, p >> 1


NT = (((1,), (1,)), ((), ()))
VMEM = pl.BlockSpec(memory_space=pltpu.VMEM)


def iota(shape, dim):
    return lax.broadcasted_iota(jnp.int32, shape, dim)


def as_column(row, n):
    eye = iota((n, n), 0) == iota((n, n), 1)
    return jnp.sum(jnp.where(eye, row, 0.0), axis=1, keepdims=True)


def as_row(column, n):
    eye = iota((n, n), 0) == iota((n, n), 1)
    return jnp.sum(jnp.where(eye, column, 0.0), axis=0, keepdims=True)


def running_sum(row, n):
    upto = jnp.where(iota((n, n), 0) <= iota((n, n), 1), 1.0, 0.0).astype(jnp.bfloat16)
    wide = jnp.broadcast_to(row, (8, n)).astype(jnp.bfloat16)
    return jnp.dot(wide, upto, preferred_element_type=F32)[0:1]


def pack_kernel(hidden_ref, target_ref, bench_ref, valid_ref, length_ref, x_ref, aux_ref):
    rows, depth = hidden_ref.shape
    kept = rows // 2
    seqs = length_ref.shape[1]
    me = lax.axis_index("d")
    ends = running_sum(length_ref[...].astype(F32), seqs).astype(jnp.int32) - 1
    position = me * rows + iota((rows, seqs), 0)
    is_end = jnp.max(jnp.where(ends == position, 1.0, 0.0), axis=1, keepdims=True)
    valid = valid_ref[...].astype(F32)
    rank = running_sum(valid, rows) - 1.0
    token = iota((1, rows), 1).astype(F32)
    count = jnp.sum(valid, axis=1, keepdims=True)
    slot = jnp.where(valid > 0.5, rank, count + token - rank - 1.0)
    selector = jnp.where(iota((kept, rows), 0).astype(F32) == slot, 1.0, 0.0).astype(jnp.bfloat16)
    scored = as_column(valid, rows) * (1.0 - is_end)
    target = target_ref[...]
    digits = [target >> 16, (target >> 8) & 255, target & 255, bench_ref[...]]
    lane = iota((rows, LAB), 1)
    labels = jnp.where(lane == 4, scored, 0.0)
    for k, digit in enumerate(digits):
        labels = jnp.where(lane == k, as_column(digit.astype(F32), rows), labels)
    x_ref[:, :depth] = jnp.dot(
        selector, hidden_ref[...], preferred_element_type=F32
    ).astype(jnp.bfloat16)
    x_ref[:, depth:] = jnp.dot(
        selector, labels.astype(jnp.bfloat16), preferred_element_type=F32
    ).astype(jnp.bfloat16)
    aux_ref[...] = jnp.where(lane == 0, as_column(slot, rows), jnp.where(lane == 1, scored, 0.0))


def pack(hidden, *ints):
    rows, depth = hidden.shape
    return pl.pallas_call(
        pack_kernel,
        out_shape=(
            jax.ShapeDtypeStruct((rows // 2, depth + LAB), jnp.bfloat16),
            jax.ShapeDtypeStruct((rows, LAB), F32),
        ),
        in_specs=[VMEM] * 5,
        out_specs=(VMEM, VMEM),
        compiler_params=pltpu.CompilerParams(vmem_limit_bytes=4 << 20),
        name="pack",
    )(hidden, *(v.reshape(1, -1) for v in ints))


def scores(x_ref, at, w_ref, acc_ref):
    vocab, depth = w_ref.shape
    r, c = iota((8, LAB), 0), iota((8, LAB), 1)
    digit = jnp.where(c == 0, 65536.0, jnp.where(c == 1, 256.0, 1.0))
    sel = jnp.where((r == 5) & (c < 3), digit, jnp.where(((r == 3) | (r == 4)) & (r == c), 1.0, 0.0))
    rows = pl.ds(at, CHUNK)
    labels = lax.dot_general(
        sel.astype(jnp.bfloat16), x_ref[rows, depth:], NT, preferred_element_type=F32
    )
    acc_ref[...] = lax.dot_general(w_ref[...], x_ref[rows, :depth], NT, preferred_element_type=F32)
    logits = acc_ref[...]
    top = jnp.max(logits, axis=0, keepdims=True)
    total = jnp.sum(jnp.exp(logits - top), axis=0, keepdims=True)
    local = labels[5:6].astype(jnp.int32) - lax.axis_index("d") * vocab
    target = jnp.sum(jnp.where(iota(logits.shape, 0) == local, logits, 0.0), axis=0, keepdims=True)
    k = iota((8, CHUNK), 0)
    return jnp.where(k == 0, top, jnp.where(k == 1, total, jnp.where(k == 2, target, labels)))


def gather_rows(pieces, x_ref):
    at = 0
    for piece in pieces:
        x_ref[at : at + piece.shape[0], :] = piece[...]
        at += piece.shape[0]


def score_kernel(w_ref, *refs):
    *pieces, out_ref, x_ref, acc_ref = refs
    gather_rows(pieces, x_ref)
    for at in range(0, x_ref.shape[0], CHUNK):
        out_ref[:, at : at + CHUNK] = scores(x_ref, at, w_ref, acc_ref)


def score(w, pieces):
    vocab, depth = w.shape
    rows = sum(p.shape[0] for p in pieces)
    return pl.pallas_call(
        score_kernel,
        out_shape=jax.ShapeDtypeStruct((8, rows), F32),
        in_specs=[VMEM] * (1 + len(pieces)),
        out_specs=VMEM,
        scratch_shapes=[
            pltpu.VMEM((rows, depth + LAB), jnp.bfloat16),
            pltpu.VMEM((vocab, CHUNK), F32),
        ],
        compiler_params=pltpu.CompilerParams(vmem_limit_bytes=LIMIT),
        cost_estimate=pl.CostEstimate(
            flops=2 * rows * vocab * depth, bytes_accessed=2 * vocab * depth, transcendentals=rows * vocab
        ),
        name="score",
    )(w, *pieces)


def score_place_kernel(w_ref, first_ref, own_ref, *refs):
    *pieces, stats_ref, labels_ref, x_ref, acc_ref, all_ref = refs
    gather_rows(pieces, x_ref)
    sib = scores(x_ref, 0, w_ref, acc_ref)
    place_of, core = coords(lax.axis_index("d"))
    bits = [cube_bits(p) for p in place_of]
    blocks = [sum(b[k] << axis for axis, b in enumerate(bits)) for k in range(2)]
    is_first = core == 0
    halves = ((first_ref[:, :CHUNK], first_ref[:, CHUNK:]), (own_ref[...], sib))
    for half, (a, b) in enumerate(halves):
        by_core = (jnp.where(is_first, a, b), jnp.where(is_first, b, a))
        for g in range(3):
            for i in range(4):
                r = 4 * half + i
                rel = sum(((r >> k) & 1) << ((g + k) % 3) for k in range(3))
                at = HALF_STARTS[g] + i * ROWS[g]
                for side in range(2):
                    to = side * 64 + STARTS[g]
                    all_ref[blocks[side] ^ rel, :, to : to + ROWS[g]] = by_core[side][:, at : at + ROWS[g]]
    for kind in range(3):
        stats_ref[kind] = all_ref[:, kind, :]
    for kind in range(2):
        labels_ref[kind] = all_ref[:, 3 + kind, :]


def score_place(w, first, own, pieces):
    vocab, depth = w.shape
    rows = sum(p.shape[0] for p in pieces)
    return pl.pallas_call(
        score_place_kernel,
        out_shape=(jax.ShapeDtypeStruct((3, 8, 128), F32), jax.ShapeDtypeStruct((2, 8, 128), F32)),
        in_specs=[VMEM] * (3 + len(pieces)),
        out_specs=(VMEM, VMEM),
        scratch_shapes=[
            pltpu.VMEM((rows, depth + LAB), jnp.bfloat16),
            pltpu.VMEM((vocab, CHUNK), F32),
            pltpu.VMEM((8, 8, 128), F32),
        ],
        compiler_params=pltpu.CompilerParams(vmem_limit_bytes=LIMIT),
        cost_estimate=pl.CostEstimate(
            flops=2 * rows * vocab * depth, bytes_accessed=2 * vocab * depth, transcendentals=rows * vocab
        ),
        name="score_place",
    )(w, first, own, *pieces)


def merged(a, b):
    best = jnp.maximum(a[0], b[0])
    total = a[1] * jnp.exp(a[0] - best) + b[1] * jnp.exp(b[0] - best)
    return best, total, a[2] + b[2]


def final_kernel(mine_ref, got_ref, labels_ref, aux_ref, loss_ref, mean_ref, count_ref, all_ref):
    best, total, target = merged(mine_ref, got_ref)
    losses = best + jnp.log(total) - target
    all_ref[...] = losses
    rows = aux_ref.shape[0]
    place_of, core = coords(lax.axis_index("d"))
    bits = [cube_bits(p) for p in place_of]
    is_first = core == 0
    block = sum(jnp.where(is_first, b[0], b[1]) << axis for axis, b in enumerate(bits))
    base = core * 64 + 8 * sum(jnp.where(is_first, b[1], b[0]) << axis for axis, b in enumerate(bits))
    mine = all_ref[pl.ds(block, 1), :]
    hit = iota((rows, LAB), 1) == base + aux_ref[:, 0:1].astype(jnp.int32)
    column = jnp.sum(jnp.where(hit, mine, 0.0), axis=1, keepdims=True)
    loss_ref[...] = as_row(column * aux_ref[:, 1:2], rows)
    bench, scored = labels_ref[0], labels_ref[1]
    kept = losses * scored
    ids = iota((BENCH, LAB), 0).astype(F32)
    sums, counts = jnp.zeros((BENCH, LAB), F32), jnp.zeros((BENCH, LAB), F32)
    for k in range(8):
        same = ids == bench[k : k + 1]
        sums += jnp.where(same, kept[k : k + 1], 0.0)
        counts += jnp.where(same, scored[k : k + 1], 0.0)
    sums = as_row(jnp.sum(sums, axis=1, keepdims=True), BENCH)
    counts = as_row(jnp.sum(counts, axis=1, keepdims=True), BENCH)
    mean_ref[...] = sums / jnp.maximum(counts, 1.0)
    count_ref[...] = counts


def final(mine, got, labels, aux):
    rows = aux.shape[0]
    outs = pl.pallas_call(
        final_kernel,
        out_shape=tuple(jax.ShapeDtypeStruct((1, n), F32) for n in (rows, BENCH, BENCH)),
        in_specs=[VMEM] * 4,
        out_specs=(VMEM,) * 3,
        scratch_shapes=[pltpu.VMEM((8, LAB), F32)],
        compiler_params=pltpu.CompilerParams(vmem_limit_bytes=4 << 20),
        name="final",
    )(mine, got, labels, aux)
    return tuple(v.reshape(-1) for v in outs)


def tied(*arrays):
    return lax.optimization_barrier(arrays)


def body(hidden, head_weight, targets, bench_ids, valid, seq_lengths):
    me = lax.axis_index("d")
    place_of, core = coords(me)
    early = [jnp.where(core == 0, b[1], b[0]) for b in map(cube_bits, place_of)]
    x, aux = pack(hidden, targets, bench_ids, valid, seq_lengths)
    for axis in range(3):
        got = exchange(x, axis, (1, 0))
        x = jnp.where(
            early[axis] == 0, jnp.concatenate([x, got], 0), jnp.concatenate([got, x], 0)
        )
    held = [x[s : s + n] for s, n in zip(STARTS, ROWS)]
    for k in range(2):
        held = tied(*held)
        got = [exchange(held[g], (g + k) % 3, (0, 1)) for g in range(3)]
        held = [jnp.concatenate([a, b], 0) for a, b in zip(held, got)]
    held = tied(*held)
    w = head_weight.T
    last = [exchange(held[g], (g + 2) % 3, (0, 1)) for g in range(3)]
    first = score(w, [*held, core_swap(jnp.concatenate(held, 0))])
    *last, first = tied(*last, first)
    other = core_swap(jnp.concatenate(last, 0))
    own = score(w, last)
    stats, labels = score_place(w, first, own, [other])
    for axis, bits in [(0, None), *((a, (b, b)) for a in range(3) for b in range(2))]:
        got = core_swap(stats) if bits is None else exchange(stats, axis, bits)
        if (axis, bits) != (2, (1, 1)):
            stats = jnp.stack(merged(stats, got))
    return final(stats, got, labels, aux)


def solution(mesh):
    flat = Mesh(mesh.devices.reshape(-1), ("d",))
    in_specs = (P("d", None), P(None, "d"), P("d"), P("d"), P("d"), P())
    return jax.shard_map(
        body, mesh=flat, in_specs=in_specs, out_specs=(P("d"), P(), P()), check_vma=False
    )
```

```python
import jax
import jax.numpy as jnp
from jax import lax
from jax.experimental import pallas as pl
from jax.experimental.pallas import tpu as pltpu
from jax.sharding import Mesh
from jax.sharding import PartitionSpec as P

BENCH = 40
N_DEV = 128
LAB = 128
ROWS = (24, 24, 16)
STARTS = (0, 24, 48)
HALF_STARTS = (0, 96, 192)
F32 = jnp.float32
CHUNK = 256
LIMIT = 12 << 20
EARLY = (((2, 0), (2, 1), (1, 0)), ((0, 0), (0, 1), (1, 1)))
LATE = (((1, 1), (0, 0), (0, 1)), ((2, 0), (2, 1), (1, 0)))


def coords(d):
    return (d // 32, (d // 4) % 4, d % 4), (d // 16) % 2


def cube_bits(p):
    return (p ^ (p >> 1)) & 1, p >> 1


def cube_index(place_of, dims):
    return sum(cube_bits(place_of[axis])[bit] << k for k, (axis, bit) in enumerate(dims))


def flipped(d, dims):
    p, core = coords(d)
    p = list(p)
    for axis, bit in dims:
        p[axis] = 3 - p[axis] if bit else p[axis] ^ 1
    return ((p[0] * 2 + core) * 4 + p[1]) * 4 + p[2]


def exchange(v, by_core):
    return lax.ppermute(v, "d", [(d, flipped(d, by_core[coords(d)[1]])) for d in range(N_DEV)])


def late_exchange(v, k):
    return exchange(v, [(dims[k % 3],) for dims in LATE])


def cross_exchange(v, dims):
    return lax.ppermute(v, "d", [(d, flipped(d, dims) ^ 16) for d in range(N_DEV)])


def core_swap(v):
    return lax.ppermute(v, "d", [(d, d ^ 16) for d in range(N_DEV)])


NT = (((1,), (1,)), ((), ()))
VMEM = pl.BlockSpec(memory_space=pltpu.VMEM)


def iota(shape, dim):
    return lax.broadcasted_iota(jnp.int32, shape, dim)


def as_column(row, n):
    eye = iota((n, n), 0) == iota((n, n), 1)
    return jnp.sum(jnp.where(eye, row, 0.0), axis=1, keepdims=True)


def as_row(column, n):
    eye = iota((n, n), 0) == iota((n, n), 1)
    return jnp.sum(jnp.where(eye, column, 0.0), axis=0, keepdims=True)


def running_sum(row, n):
    upto = jnp.where(iota((n, n), 0) <= iota((n, n), 1), 1.0, 0.0).astype(jnp.bfloat16)
    wide = jnp.broadcast_to(row, (8, n)).astype(jnp.bfloat16)
    return jnp.dot(wide, upto, preferred_element_type=F32)[0:1]


def pack_kernel(hidden_ref, ints_ref, x_ref, aux_ref):
    rows, depth = hidden_ref.shape
    kept = rows // 2
    ints = ints_ref[...]
    target, bench, valid = (ints[:, k * rows : (k + 1) * rows] for k in range(3))
    lengths = ints[:, 3 * rows :]
    seqs = lengths.shape[1]
    me = lax.axis_index("d")
    ends = running_sum(lengths.astype(F32), seqs).astype(jnp.int32) - 1
    position = me * rows + iota((rows, seqs), 0)
    is_end = jnp.max(jnp.where(ends == position, 1.0, 0.0), axis=1, keepdims=True)
    valid = valid.astype(F32)
    rank = running_sum(valid, rows) - 1.0
    token = iota((1, rows), 1).astype(F32)
    count = jnp.sum(valid, axis=1, keepdims=True)
    slot = jnp.where(valid > 0.5, rank, count + token - rank - 1.0)
    selector = jnp.where(iota((kept, rows), 0).astype(F32) == slot, 1.0, 0.0).astype(jnp.bfloat16)
    scored = as_column(valid, rows) * (1.0 - is_end)
    digits = [target >> 16, (target >> 8) & 255, target & 255, bench]
    lane = iota((rows, LAB), 1)
    labels = jnp.where(lane == 4, scored, 0.0)
    for k, digit in enumerate(digits):
        labels = jnp.where(lane == k, as_column(digit.astype(F32), rows), labels)
    x_ref[:, :depth] = jnp.dot(
        selector, hidden_ref[...], preferred_element_type=F32
    ).astype(jnp.bfloat16)
    x_ref[:, depth:] = jnp.dot(
        selector, labels.astype(jnp.bfloat16), preferred_element_type=F32
    ).astype(jnp.bfloat16)
    aux_ref[...] = jnp.where(lane == 0, as_column(slot, rows), jnp.where(lane == 1, scored, 0.0))


def pack(hidden, *ints):
    rows, depth = hidden.shape
    return pl.pallas_call(
        pack_kernel,
        out_shape=(
            jax.ShapeDtypeStruct((rows // 2, depth + LAB), jnp.bfloat16),
            jax.ShapeDtypeStruct((rows, LAB), F32),
        ),
        in_specs=[VMEM, VMEM],
        out_specs=(VMEM, VMEM),
        compiler_params=pltpu.CompilerParams(vmem_limit_bytes=4 << 20),
        name="pack",
    )(hidden, jnp.concatenate(ints).reshape(1, -1))


def scores(x_ref, at, w_ref, acc_ref):
    vocab, depth = w_ref.shape
    r, c = iota((8, LAB), 0), iota((8, LAB), 1)
    digit = jnp.where(c == 0, 65536.0, jnp.where(c == 1, 256.0, 1.0))
    sel = jnp.where((r == 5) & (c < 3), digit, jnp.where(((r == 3) | (r == 4)) & (r == c), 1.0, 0.0))
    rows = pl.ds(at, CHUNK)
    labels = lax.dot_general(
        sel.astype(jnp.bfloat16), x_ref[rows, depth:], NT, preferred_element_type=F32
    )
    acc_ref[...] = lax.dot_general(w_ref[...], x_ref[rows, :depth], NT, preferred_element_type=F32)
    logits = acc_ref[...]
    top = jnp.max(logits, axis=0, keepdims=True)
    total = jnp.sum(jnp.exp(logits - top), axis=0, keepdims=True)
    local = labels[5:6].astype(jnp.int32) - lax.axis_index("d") * vocab
    target = jnp.sum(jnp.where(iota(logits.shape, 0) == local, logits, 0.0), axis=0, keepdims=True)
    k = iota((8, CHUNK), 0)
    return jnp.where(k == 0, top, jnp.where(k == 1, total, jnp.where(k == 2, target, labels)))


def gather_rows(pieces, x_ref):
    at = 0
    for piece in pieces:
        x_ref[at : at + piece.shape[0], :] = piece[...]
        at += piece.shape[0]


def score_kernel(w_ref, *refs):
    *pieces, out_ref, x_ref, acc_ref = refs
    gather_rows(pieces, x_ref)
    for at in range(0, x_ref.shape[0], CHUNK):
        out_ref[:, at : at + CHUNK] = scores(x_ref, at, w_ref, acc_ref)


def score(w, pieces):
    vocab, depth = w.shape
    rows = sum(p.shape[0] for p in pieces)
    return pl.pallas_call(
        score_kernel,
        out_shape=jax.ShapeDtypeStruct((8, rows), F32),
        in_specs=[VMEM] * (1 + len(pieces)),
        out_specs=VMEM,
        scratch_shapes=[
            pltpu.VMEM((rows, depth + LAB), jnp.bfloat16),
            pltpu.VMEM((vocab, CHUNK), F32),
        ],
        compiler_params=pltpu.CompilerParams(vmem_limit_bytes=LIMIT),
        cost_estimate=pl.CostEstimate(
            flops=2 * rows * vocab * depth, bytes_accessed=2 * vocab * depth, transcendentals=rows * vocab
        ),
        name="score",
    )(w, *pieces)


def score_place_kernel(w_ref, first_ref, own_ref, *refs):
    *pieces, stats_ref, labels_ref, x_ref, acc_ref, all_ref = refs
    gather_rows(pieces, x_ref)
    sib = scores(x_ref, 0, w_ref, acc_ref)
    place_of, core = coords(lax.axis_index("d"))
    blocks = [cube_index(place_of, LATE[k]) for k in range(2)]
    is_first = core == 0
    halves = ((first_ref[:, :CHUNK], first_ref[:, CHUNK:]), (own_ref[...], sib))
    for half, (a, b) in enumerate(halves):
        by_core = (jnp.where(is_first, a, b), jnp.where(is_first, b, a))
        for g in range(3):
            for i in range(4):
                r = 4 * half + i
                rel = sum(((r >> k) & 1) << ((g + k) % 3) for k in range(3))
                at = HALF_STARTS[g] + i * ROWS[g]
                for side in range(2):
                    to = side * 64 + STARTS[g]
                    all_ref[blocks[side] ^ rel, :, to : to + ROWS[g]] = by_core[side][:, at : at + ROWS[g]]
    for kind in range(3):
        stats_ref[kind] = all_ref[:, kind, :]
    for kind in range(2):
        labels_ref[kind] = all_ref[:, 3 + kind, :]


def score_place(w, first, own, pieces):
    vocab, depth = w.shape
    rows = sum(p.shape[0] for p in pieces)
    return pl.pallas_call(
        score_place_kernel,
        out_shape=(jax.ShapeDtypeStruct((3, 8, 128), F32), jax.ShapeDtypeStruct((2, 8, 128), F32)),
        in_specs=[VMEM] * (3 + len(pieces)),
        out_specs=(VMEM, VMEM),
        scratch_shapes=[
            pltpu.VMEM((rows, depth + LAB), jnp.bfloat16),
            pltpu.VMEM((vocab, CHUNK), F32),
            pltpu.VMEM((8, 8, 128), F32),
        ],
        compiler_params=pltpu.CompilerParams(vmem_limit_bytes=LIMIT),
        cost_estimate=pl.CostEstimate(
            flops=2 * rows * vocab * depth, bytes_accessed=2 * vocab * depth, transcendentals=rows * vocab
        ),
        name="score_place",
    )(w, first, own, *pieces)


def merged(parts):
    best = parts[0][0]
    for p in parts[1:]:
        best = jnp.maximum(best, p[0])
    total = sum(p[1] * jnp.exp(p[0] - best) for p in parts)
    return best, total, sum(p[2] for p in parts)


def final_kernel(*refs):
    *parts, labels_ref, aux_ref, loss_ref, mean_ref, count_ref, all_ref = refs
    best, total, target = merged(parts)
    losses = best + jnp.log(total) - target
    all_ref[...] = losses
    rows = aux_ref.shape[0]
    place_of, core = coords(lax.axis_index("d"))
    block = jnp.where(core == 0, *(cube_index(place_of, dims) for dims in LATE))
    base = core * 64 + 8 * jnp.where(core == 0, *(cube_index(place_of, dims) for dims in EARLY))
    mine = all_ref[pl.ds(block, 1), :]
    hit = iota((rows, LAB), 1) == base + aux_ref[:, 0:1].astype(jnp.int32)
    column = jnp.sum(jnp.where(hit, mine, 0.0), axis=1, keepdims=True)
    loss_ref[...] = as_row(column * aux_ref[:, 1:2], rows)
    bench, scored = labels_ref[0], labels_ref[1]
    kept = losses * scored
    ids = iota((BENCH, LAB), 0).astype(F32)
    sums, counts = jnp.zeros((BENCH, LAB), F32), jnp.zeros((BENCH, LAB), F32)
    for k in range(8):
        same = ids == bench[k : k + 1]
        sums += jnp.where(same, kept[k : k + 1], 0.0)
        counts += jnp.where(same, scored[k : k + 1], 0.0)
    sums = as_row(jnp.sum(sums, axis=1, keepdims=True), BENCH)
    counts = as_row(jnp.sum(counts, axis=1, keepdims=True), BENCH)
    mean_ref[...] = sums / jnp.maximum(counts, 1.0)
    count_ref[...] = counts


def final(parts, labels, aux):
    rows = aux.shape[0]
    outs = pl.pallas_call(
        final_kernel,
        out_shape=tuple(jax.ShapeDtypeStruct((1, n), F32) for n in (rows, BENCH, BENCH)),
        in_specs=[VMEM] * (len(parts) + 2),
        out_specs=(VMEM,) * 3,
        scratch_shapes=[pltpu.VMEM((8, LAB), F32)],
        compiler_params=pltpu.CompilerParams(vmem_limit_bytes=4 << 20),
        name="final",
    )(*parts, labels, aux)
    return tuple(v.reshape(-1) for v in outs)


def tied(*arrays):
    return lax.optimization_barrier(arrays)


def ordered(low, a, b):
    return jnp.where(low, jnp.concatenate([a, b], 0), jnp.concatenate([b, a], 0))


def body(hidden, head_weight, targets, bench_ids, valid, seq_lengths):
    place_of, core = coords(lax.axis_index("d"))
    early = jnp.where(core == 0, *(cube_index(place_of, dims) for dims in EARLY))
    low = [(early >> k) & 1 == 0 for k in range(3)]
    x, aux = pack(hidden, targets, bench_ids, valid, seq_lengths)
    both, first, second = (exchange(x, [d[s] for d in EARLY]) for s in (slice(0, 2), slice(0, 1), slice(1, 2)))
    x = ordered(low[1], ordered(low[0], x, first), ordered(low[0], second, both))
    x = ordered(low[2], x, exchange(x, [d[2:] for d in EARLY]))
    held = tied(*(x[s : s + n] for s, n in zip(STARTS, ROWS)))
    for k in range(2):
        got = [late_exchange(held[g], g + k) for g in range(3)]
        held = [jnp.concatenate([a, b], 0) for a, b in zip(held, got)]
    w = head_weight.T
    last = [late_exchange(held[g], g + 2) for g in range(3)]
    first = score(w, [*held, core_swap(jnp.concatenate(held, 0))])
    *last, first = tied(*last, first)
    other = core_swap(jnp.concatenate(last, 0))
    own = score(w, last)
    stats, labels = score_place(w, first, own, [other])
    parts = [stats, core_swap(stats)]
    for axis in range(3):
        stats = jnp.stack(merged(parts))
        steps = [(axis, 0), (axis, 1)]
        parts = [stats, *(cross_exchange(stats, d) for d in (steps[:1], steps[1:], steps))]
    return final(parts, labels, aux)


def solution(mesh):
    flat = Mesh(mesh.devices.reshape(-1), ("d",))
    in_specs = (P("d", None), P(None, "d"), P("d"), P("d"), P("d"), P())
    return jax.shard_map(
        body, mesh=flat, in_specs=in_specs, out_specs=(P("d"), P(), P()), check_vma=False
    )
```

```python
import jax
import jax.numpy as jnp
from jax import lax
from jax.experimental import pallas as pl
from jax.experimental.pallas import tpu as pltpu
from jax.sharding import Mesh
from jax.sharding import PartitionSpec as P

BENCH = 40
N_DEV = 128
LAB = 128
CUTS = (0, 32, 64)
SETS = ((0, 1, 2, 4), (3, 6, 5), (7,))
F32 = jnp.float32
LIMIT = 12 << 20
BLOCK = 64
EARLY = (((2, 0), (2, 1), (1, 0)), ((0, 0), (0, 1), (1, 1)))
LATE = (((1, 1), (0, 0), (0, 1)), ((2, 0), (2, 1), (1, 0)))


def coords(d):
    return (d // 32, (d // 4) % 4, d % 4), (d // 16) % 2


def cube_bits(p):
    return (p ^ (p >> 1)) & 1, p >> 1


def cube_index(place_of, dims):
    return sum(cube_bits(place_of[axis])[bit] << k for k, (axis, bit) in enumerate(dims))


def flipped(d, dims):
    p, core = coords(d)
    p = list(p)
    for axis, bit in dims:
        p[axis] = 3 - p[axis] if bit else p[axis] ^ 1
    return ((p[0] * 2 + core) * 4 + p[1]) * 4 + p[2]


def exchange(v, by_core):
    return lax.ppermute(v, "d", [(d, flipped(d, by_core[coords(d)[1]])) for d in range(N_DEV)])


def late_exchange(v, k):
    return exchange(v, [(dims[k % 3],) for dims in LATE])


def cross_exchange(v, dims):
    return lax.ppermute(v, "d", [(d, flipped(d, dims) ^ 16) for d in range(N_DEV)])


def core_swap(v):
    return lax.ppermute(v, "d", [(d, d ^ 16) for d in range(N_DEV)])


NT = (((1,), (1,)), ((), ()))
VMEM = pl.BlockSpec(memory_space=pltpu.VMEM)


def iota(shape, dim):
    return lax.broadcasted_iota(jnp.int32, shape, dim)


def as_column(row, n):
    eye = iota((n, n), 0) == iota((n, n), 1)
    return jnp.sum(jnp.where(eye, row, 0.0), axis=1, keepdims=True)


def as_row(column, n):
    eye = iota((n, n), 0) == iota((n, n), 1)
    return jnp.sum(jnp.where(eye, column, 0.0), axis=0, keepdims=True)


def running_sum(row, n):
    upto = jnp.where(iota((n, n), 0) <= iota((n, n), 1), 1.0, 0.0).astype(jnp.bfloat16)
    wide = jnp.broadcast_to(row, (8, n)).astype(jnp.bfloat16)
    return jnp.dot(wide, upto, preferred_element_type=F32)[0:1]


def pack_kernel(hidden_ref, ints_ref, x_ref, aux_ref):
    rows, depth = hidden_ref.shape
    kept = rows // 2
    ints = ints_ref[...]
    target, bench, valid = (ints[:, k * rows : (k + 1) * rows] for k in range(3))
    lengths = ints[:, 3 * rows :]
    seqs = lengths.shape[1]
    me = lax.axis_index("d")
    ends = running_sum(lengths.astype(F32), seqs).astype(jnp.int32) - 1
    position = me * rows + iota((rows, seqs), 0)
    is_end = jnp.max(jnp.where(ends == position, 1.0, 0.0), axis=1, keepdims=True)
    valid = valid.astype(F32)
    rank = running_sum(valid, rows) - 1.0
    token = iota((1, rows), 1).astype(F32)
    count = jnp.sum(valid, axis=1, keepdims=True)
    slot = jnp.where(valid > 0.5, rank, count + token - rank - 1.0)
    selector = jnp.where(iota((kept, rows), 0).astype(F32) == slot, 1.0, 0.0).astype(jnp.bfloat16)
    scored = as_column(valid, rows) * (1.0 - is_end)
    digits = [target >> 16, (target >> 8) & 255, target & 255, bench]
    lane = iota((rows, LAB), 1)
    labels = jnp.where(lane == 4, scored, 0.0)
    for k, digit in enumerate(digits):
        labels = jnp.where(lane == k, as_column(digit.astype(F32), rows), labels)
    x_ref[:, :depth] = jnp.dot(
        selector, hidden_ref[...], preferred_element_type=F32
    ).astype(jnp.bfloat16)
    x_ref[:, depth:] = jnp.dot(
        selector, labels.astype(jnp.bfloat16), preferred_element_type=F32
    ).astype(jnp.bfloat16)
    aux_ref[...] = jnp.where(lane == 0, as_column(slot, rows), jnp.where(lane == 1, scored, 0.0))


def pack(hidden, *ints):
    rows, depth = hidden.shape
    return pl.pallas_call(
        pack_kernel,
        out_shape=(
            jax.ShapeDtypeStruct((rows // 2, depth + LAB), jnp.bfloat16),
            jax.ShapeDtypeStruct((rows, LAB), F32),
        ),
        in_specs=[VMEM, VMEM],
        out_specs=(VMEM, VMEM),
        compiler_params=pltpu.CompilerParams(vmem_limit_bytes=4 << 20),
        name="pack",
    )(hidden, jnp.concatenate(ints).reshape(1, -1))


def scores(x_ref, w_ref, acc_ref):
    vocab, depth = w_ref.shape
    r, c = iota((8, LAB), 0), iota((8, LAB), 1)
    digit = jnp.where(c == 0, 65536.0, jnp.where(c == 1, 256.0, 1.0))
    sel = jnp.where((r == 5) & (c < 3), digit, jnp.where(((r == 3) | (r == 4)) & (r == c), 1.0, 0.0))
    labels = lax.dot_general(
        sel.astype(jnp.bfloat16), x_ref[:, depth:], NT, preferred_element_type=F32
    )
    acc_ref[...] = lax.dot_general(w_ref[...], x_ref[:, :depth], NT, preferred_element_type=F32)
    logits = acc_ref[...]
    top = jnp.max(logits, axis=0, keepdims=True)
    total = jnp.sum(jnp.exp(logits - top), axis=0, keepdims=True)
    local = labels[5:6].astype(jnp.int32) - lax.axis_index("d") * vocab
    target = jnp.sum(jnp.where(iota(logits.shape, 0) == local, logits, 0.0), axis=0, keepdims=True)
    k = iota((8, x_ref.shape[0]), 0)
    return jnp.where(k == 0, top, jnp.where(k == 1, total, jnp.where(k == 2, target, labels)))


def gather_rows(pieces, x_ref):
    at = 0
    for piece in pieces:
        x_ref[at : at + piece.shape[0], :] = piece[...]
        at += piece.shape[0]


def score_kernel(w_ref, *refs):
    *pieces, out_ref, x_ref, acc_ref = refs
    gather_rows(pieces, x_ref)
    out_ref[...] = scores(x_ref, w_ref, acc_ref)


def score(w, pieces):
    vocab, depth = w.shape
    rows = sum(p.shape[0] for p in pieces)
    return pl.pallas_call(
        score_kernel,
        out_shape=jax.ShapeDtypeStruct((8, rows), F32),
        in_specs=[VMEM] * (1 + len(pieces)),
        out_specs=VMEM,
        scratch_shapes=[
            pltpu.VMEM((rows, depth + LAB), jnp.bfloat16),
            pltpu.VMEM((vocab, rows), F32),
        ],
        compiler_params=pltpu.CompilerParams(vmem_limit_bytes=LIMIT),
        cost_estimate=pl.CostEstimate(
            flops=2 * rows * vocab * depth, bytes_accessed=2 * vocab * depth, transcendentals=rows * vocab
        ),
        name="score",
    )(w, *pieces)


def score_place_kernel(w_ref, *refs):
    *refs, stats_ref, labels_ref, x_ref, acc_ref, all_ref = refs
    done, pieces = refs[:4], refs[4:]
    gather_rows(pieces, x_ref)
    last = scores(x_ref, w_ref, acc_ref)
    place_of, core = coords(lax.axis_index("d"))
    blocks = [cube_index(place_of, LATE[k]) for k in range(2)]
    is_first = core == 0
    pairs = [(done[0][...], done[1][...]), (done[2][...], done[3][...]), (last[:, :BLOCK], last[:, BLOCK:])]
    for rels, (own, sib) in zip(SETS, pairs):
        by_core = (jnp.where(is_first, own, sib), jnp.where(is_first, sib, own))
        for i, rel in enumerate(rels):
            for side in range(2):
                to = side * BLOCK
                all_ref[blocks[side] ^ rel, :, to : to + BLOCK] = by_core[side][:, i * BLOCK : (i + 1) * BLOCK]
    for kind in range(3):
        stats_ref[kind] = all_ref[:, kind, :]
    for kind in range(2):
        labels_ref[kind] = all_ref[:, 3 + kind, :]


def score_place(w, done, pieces):
    vocab, depth = w.shape
    rows = sum(p.shape[0] for p in pieces)
    return pl.pallas_call(
        score_place_kernel,
        out_shape=(jax.ShapeDtypeStruct((3, 8, 128), F32), jax.ShapeDtypeStruct((2, 8, 128), F32)),
        in_specs=[VMEM] * (1 + len(done) + len(pieces)),
        out_specs=(VMEM, VMEM),
        scratch_shapes=[
            pltpu.VMEM((rows, depth + LAB), jnp.bfloat16),
            pltpu.VMEM((vocab, rows), F32),
            pltpu.VMEM((8, 8, 128), F32),
        ],
        compiler_params=pltpu.CompilerParams(vmem_limit_bytes=LIMIT),
        cost_estimate=pl.CostEstimate(
            flops=2 * rows * vocab * depth, bytes_accessed=2 * vocab * depth, transcendentals=rows * vocab
        ),
        name="score_place",
    )(w, *done, *pieces)


def merged(parts):
    best = parts[0][0]
    for p in parts[1:]:
        best = jnp.maximum(best, p[0])
    total = sum(p[1] * jnp.exp(p[0] - best) for p in parts)
    return best, total, sum(p[2] for p in parts)


def final_kernel(*refs):
    *parts, labels_ref, aux_ref, loss_ref, mean_ref, count_ref, all_ref = refs
    best, total, target = merged(parts)
    losses = best + jnp.log(total) - target
    all_ref[...] = losses
    rows = aux_ref.shape[0]
    place_of, core = coords(lax.axis_index("d"))
    block = jnp.where(core == 0, *(cube_index(place_of, dims) for dims in LATE))
    base = core * 64 + 8 * jnp.where(core == 0, *(cube_index(place_of, dims) for dims in EARLY))
    mine = all_ref[pl.ds(block, 1), :]
    hit = iota((rows, LAB), 1) == base + aux_ref[:, 0:1].astype(jnp.int32)
    column = jnp.sum(jnp.where(hit, mine, 0.0), axis=1, keepdims=True)
    loss_ref[...] = as_row(column * aux_ref[:, 1:2], rows)
    bench, scored = labels_ref[0], labels_ref[1]
    kept = losses * scored
    ids = iota((BENCH, LAB), 0).astype(F32)
    sums, counts = jnp.zeros((BENCH, LAB), F32), jnp.zeros((BENCH, LAB), F32)
    for k in range(8):
        same = ids == bench[k : k + 1]
        sums += jnp.where(same, kept[k : k + 1], 0.0)
        counts += jnp.where(same, scored[k : k + 1], 0.0)
    sums = as_row(jnp.sum(sums, axis=1, keepdims=True), BENCH)
    counts = as_row(jnp.sum(counts, axis=1, keepdims=True), BENCH)
    mean_ref[...] = sums / jnp.maximum(counts, 1.0)
    count_ref[...] = counts


def final(parts, labels, aux):
    rows = aux.shape[0]
    outs = pl.pallas_call(
        final_kernel,
        out_shape=tuple(jax.ShapeDtypeStruct((1, n), F32) for n in (rows, BENCH, BENCH)),
        in_specs=[VMEM] * (len(parts) + 2),
        out_specs=(VMEM,) * 3,
        scratch_shapes=[pltpu.VMEM((8, LAB), F32)],
        compiler_params=pltpu.CompilerParams(vmem_limit_bytes=4 << 20),
        name="final",
    )(*parts, labels, aux)
    return tuple(v.reshape(-1) for v in outs)


def tied(*arrays):
    return lax.optimization_barrier(arrays)


def fetch_kernel(w_ref, out_ref, sem):
    move = pltpu.make_async_copy(w_ref, out_ref, sem)
    move.start()
    move.wait()


def fetch(w):
    return pl.pallas_call(
        fetch_kernel,
        out_shape=jax.ShapeDtypeStruct(w.shape, w.dtype),
        in_specs=[pl.BlockSpec(memory_space=pl.ANY)],
        out_specs=VMEM,
        scratch_shapes=[pltpu.SemaphoreType.DMA],
        compiler_params=pltpu.CompilerParams(vmem_limit_bytes=LIMIT),
        cost_estimate=pl.CostEstimate(flops=0, bytes_accessed=2 * w.size, transcendentals=0),
        name="fetch",
    )(w)


def ordered(low, a, b):
    return jnp.where(low, jnp.concatenate([a, b], 0), jnp.concatenate([b, a], 0))


def body(hidden, head_weight, targets, bench_ids, valid, seq_lengths):
    place_of, core = coords(lax.axis_index("d"))
    early = jnp.where(core == 0, *(cube_index(place_of, dims) for dims in EARLY))
    low = [(early >> k) & 1 == 0 for k in range(3)]
    x, aux = pack(hidden, targets, bench_ids, valid, seq_lengths)
    both, first, second = (exchange(x, [d[s] for d in EARLY]) for s in (slice(0, 2), slice(0, 1), slice(1, 2)))
    x = ordered(low[1], ordered(low[0], x, first), ordered(low[0], second, both))
    x = ordered(low[2], x, exchange(x, [d[2:] for d in EARLY]))
    x, w = tied(x, fetch(head_weight.T))
    near = [late_exchange(x, k) for k in range(3)]
    near_rows = [x, *near]
    own1 = score(w, near_rows)
    sib1 = score(w, [core_swap(jnp.concatenate(near_rows, 0))])
    far = [late_exchange(near[(k + 1) % 3], k) for k in range(3)]
    *far, own1, sib1 = tied(*far, own1, sib1)
    own2 = score(w, far)
    sib2 = score(w, [core_swap(jnp.concatenate(far, 0))])
    spans = zip(CUTS, CUTS[1:])
    last = jnp.concatenate(
        [late_exchange(far[(k + 1) % 3][i:j], k) for k, (i, j) in enumerate(spans)], 0
    )
    last, own2 = tied(last, own2)
    stats, labels = score_place(w, (own1, sib1, own2, sib2), [last, core_swap(last)])
    parts = [stats, core_swap(stats)]
    for axis in range(3):
        stats = jnp.stack(merged(parts))
        steps = [(axis, 0), (axis, 1)]
        parts = [stats, *(cross_exchange(stats, d) for d in (steps[:1], steps[1:], steps))]
    return final(parts, labels, aux)


def solution(mesh):
    flat = Mesh(mesh.devices.reshape(-1), ("d",))
    in_specs = (P("d", None), P(None, "d"), P("d"), P("d"), P("d"), P())
    return jax.shard_map(
        body, mesh=flat, in_specs=in_specs, out_specs=(P("d"), P(), P()), check_vma=False
    )
```

```python
import jax
import jax.numpy as jnp
from jax import lax
from jax.experimental import pallas as pl
from jax.experimental.pallas import tpu as pltpu
from jax.sharding import Mesh
from jax.sharding import PartitionSpec as P

BENCH = 40
N_DEV = 128
LAB = 128
CUTS = (0, 32, 64)
SETS = ((0, 1, 2, 4), (3, 6, 5), (7,))
F32 = jnp.float32
LIMIT = 12 << 20
BLOCK = 64
EARLY = (((2, 0), (1, 0), (0, 0)), ((2, 1), (1, 1), (0, 1)))
LATE = (EARLY[1], EARLY[0])


def coords(d):
    return (d // 32, (d // 4) % 4, d % 4), (d // 16) % 2


def cube_bits(p):
    return (p ^ (p >> 1)) & 1, p >> 1


def cube_index(place_of, dims):
    return sum(cube_bits(place_of[axis])[bit] << k for k, (axis, bit) in enumerate(dims))


def flipped(d, dims):
    p, core = coords(d)
    p = list(p)
    for axis, bit in dims:
        p[axis] = 3 - p[axis] if bit else p[axis] ^ 1
    return ((p[0] * 2 + core) * 4 + p[1]) * 4 + p[2]


def exchange(v, by_core):
    return lax.ppermute(v, "d", [(d, flipped(d, by_core[coords(d)[1]])) for d in range(N_DEV)])


def late_exchange(v, k):
    return exchange(v, [(dims[k % 3],) for dims in LATE])


def cross_exchange(v, dims):
    return lax.ppermute(v, "d", [(d, flipped(d, dims) ^ 16) for d in range(N_DEV)])


def early_groups():
    groups = {}
    for d in range(N_DEV):
        p, core = coords(d)
        groups.setdefault((core, cube_index(p, LATE[core])), []).append((cube_index(p, EARLY[core]), d))
    return [[d for _, d in sorted(group)] for group in groups.values()]


def core_swap(v):
    return lax.ppermute(v, "d", [(d, d ^ 16) for d in range(N_DEV)])


NT = (((1,), (1,)), ((), ()))
VMEM = pl.BlockSpec(memory_space=pltpu.VMEM)


def iota(shape, dim):
    return lax.broadcasted_iota(jnp.int32, shape, dim)


def as_column(row, n):
    eye = iota((n, n), 0) == iota((n, n), 1)
    return jnp.sum(jnp.where(eye, row, 0.0), axis=1, keepdims=True)


def as_row(column, n):
    eye = iota((n, n), 0) == iota((n, n), 1)
    return jnp.sum(jnp.where(eye, column, 0.0), axis=0, keepdims=True)


def running_sum(row, n):
    upto = jnp.where(iota((n, n), 0) <= iota((n, n), 1), 1.0, 0.0).astype(jnp.bfloat16)
    wide = jnp.broadcast_to(row, (8, n)).astype(jnp.bfloat16)
    return jnp.dot(wide, upto, preferred_element_type=F32)[0:1]


def pack_kernel(hidden_ref, ints_ref, x_ref, aux_ref):
    rows, depth = hidden_ref.shape
    kept = rows // 2
    ints = ints_ref[...]
    target, bench, valid = (ints[:, k * rows : (k + 1) * rows] for k in range(3))
    lengths = ints[:, 3 * rows :]
    seqs = lengths.shape[1]
    me = lax.axis_index("d")
    ends = running_sum(lengths.astype(F32), seqs).astype(jnp.int32) - 1
    position = me * rows + iota((rows, seqs), 0)
    is_end = jnp.max(jnp.where(ends == position, 1.0, 0.0), axis=1, keepdims=True)
    valid = valid.astype(F32)
    rank = running_sum(valid, rows) - 1.0
    token = iota((1, rows), 1).astype(F32)
    count = jnp.sum(valid, axis=1, keepdims=True)
    slot = jnp.where(valid > 0.5, rank, count + token - rank - 1.0)
    selector = jnp.where(iota((kept, rows), 0).astype(F32) == slot, 1.0, 0.0).astype(jnp.bfloat16)
    scored = as_column(valid, rows) * (1.0 - is_end)
    digits = [target >> 16, (target >> 8) & 255, target & 255, bench]
    lane = iota((rows, LAB), 1)
    labels = jnp.where(lane == 4, scored, 0.0)
    for k, digit in enumerate(digits):
        labels = jnp.where(lane == k, as_column(digit.astype(F32), rows), labels)
    picked = jnp.dot(selector, hidden_ref[...], preferred_element_type=F32).astype(jnp.bfloat16)
    tags = jnp.dot(selector, labels.astype(jnp.bfloat16), preferred_element_type=F32).astype(jnp.bfloat16)
    for k in range(x_ref.shape[0]):
        x_ref[k, :, :depth] = picked
        x_ref[k, :, depth:] = tags
    aux_ref[...] = jnp.where(lane == 0, as_column(slot, rows), jnp.where(lane == 1, scored, 0.0))


def pack(hidden, *ints):
    rows, depth = hidden.shape
    return pl.pallas_call(
        pack_kernel,
        out_shape=(
            jax.ShapeDtypeStruct((8, rows // 2, depth + LAB), jnp.bfloat16),
            jax.ShapeDtypeStruct((rows, LAB), F32),
        ),
        in_specs=[VMEM, VMEM],
        out_specs=(VMEM, VMEM),
        compiler_params=pltpu.CompilerParams(vmem_limit_bytes=4 << 20),
        name="pack",
    )(hidden, jnp.concatenate(ints).reshape(1, -1))


def scores(x_ref, w_ref, acc_ref):
    vocab, depth = w_ref.shape
    r, c = iota((8, LAB), 0), iota((8, LAB), 1)
    digit = jnp.where(c == 0, 65536.0, jnp.where(c == 1, 256.0, 1.0))
    sel = jnp.where((r == 5) & (c < 3), digit, jnp.where(((r == 3) | (r == 4)) & (r == c), 1.0, 0.0))
    labels = lax.dot_general(
        sel.astype(jnp.bfloat16), x_ref[:, depth:], NT, preferred_element_type=F32
    )
    acc_ref[...] = lax.dot_general(w_ref[...], x_ref[:, :depth], NT, preferred_element_type=F32)
    logits = acc_ref[...]
    top = jnp.max(logits, axis=0, keepdims=True)
    total = jnp.sum(jnp.exp(logits - top), axis=0, keepdims=True)
    local = labels[5:6].astype(jnp.int32) - lax.axis_index("d") * vocab
    target = jnp.sum(jnp.where(iota(logits.shape, 0) == local, logits, 0.0), axis=0, keepdims=True)
    k = iota((8, x_ref.shape[0]), 0)
    return jnp.where(k == 0, top, jnp.where(k == 1, total, jnp.where(k == 2, target, labels)))


def gather_rows(pieces, x_ref):
    at = 0
    for piece in pieces:
        x_ref[at : at + piece.shape[0], :] = piece[...]
        at += piece.shape[0]


def score_kernel(w_ref, *refs):
    *pieces, out_ref, x_ref, acc_ref = refs
    gather_rows(pieces, x_ref)
    out_ref[...] = scores(x_ref, w_ref, acc_ref)


def score(w, pieces):
    vocab, depth = w.shape
    rows = sum(p.shape[0] for p in pieces)
    return pl.pallas_call(
        score_kernel,
        out_shape=jax.ShapeDtypeStruct((8, rows), F32),
        in_specs=[VMEM] * (1 + len(pieces)),
        out_specs=VMEM,
        scratch_shapes=[
            pltpu.VMEM((rows, depth + LAB), jnp.bfloat16),
            pltpu.VMEM((vocab, rows), F32),
        ],
        compiler_params=pltpu.CompilerParams(vmem_limit_bytes=LIMIT),
        cost_estimate=pl.CostEstimate(
            flops=2 * rows * vocab * depth, bytes_accessed=2 * vocab * depth, transcendentals=rows * vocab
        ),
        name="score",
    )(w, *pieces)


def score_place_kernel(w_ref, *refs):
    *refs, stats_ref, labels_ref, x_ref, acc_ref, all_ref = refs
    done, pieces = refs[:4], refs[4:]
    gather_rows(pieces, x_ref)
    last = scores(x_ref, w_ref, acc_ref)
    place_of, core = coords(lax.axis_index("d"))
    blocks = [cube_index(place_of, LATE[k]) for k in range(2)]
    is_first = core == 0
    pairs = [(done[0][...], done[1][...]), (done[2][...], done[3][...]), (last[:, :BLOCK], last[:, BLOCK:])]
    for rels, (own, sib) in zip(SETS, pairs):
        by_core = (jnp.where(is_first, own, sib), jnp.where(is_first, sib, own))
        for i, rel in enumerate(rels):
            for side in range(2):
                to = side * BLOCK
                all_ref[blocks[side] ^ rel, :, to : to + BLOCK] = by_core[side][:, i * BLOCK : (i + 1) * BLOCK]
    for kind in range(3):
        stats_ref[kind] = all_ref[:, kind, :]
    for kind in range(2):
        labels_ref[kind] = all_ref[:, 3 + kind, :]


def score_place(w, done, pieces):
    vocab, depth = w.shape
    rows = sum(p.shape[0] for p in pieces)
    return pl.pallas_call(
        score_place_kernel,
        out_shape=(jax.ShapeDtypeStruct((3, 8, 128), F32), jax.ShapeDtypeStruct((2, 8, 128), F32)),
        in_specs=[VMEM] * (1 + len(done) + len(pieces)),
        out_specs=(VMEM, VMEM),
        scratch_shapes=[
            pltpu.VMEM((rows, depth + LAB), jnp.bfloat16),
            pltpu.VMEM((vocab, rows), F32),
            pltpu.VMEM((8, 8, 128), F32),
        ],
        compiler_params=pltpu.CompilerParams(vmem_limit_bytes=LIMIT),
        cost_estimate=pl.CostEstimate(
            flops=2 * rows * vocab * depth, bytes_accessed=2 * vocab * depth, transcendentals=rows * vocab
        ),
        name="score_place",
    )(w, *done, *pieces)


def merged(parts):
    best = parts[0][0]
    for p in parts[1:]:
        best = jnp.maximum(best, p[0])
    total = sum(p[1] * jnp.exp(p[0] - best) for p in parts)
    return best, total, sum(p[2] for p in parts)


def final_kernel(*refs):
    *parts, labels_ref, aux_ref, loss_ref, mean_ref, count_ref, all_ref = refs
    best, total, target = merged(parts)
    losses = best + jnp.log(total) - target
    all_ref[...] = losses
    rows = aux_ref.shape[0]
    place_of, core = coords(lax.axis_index("d"))
    block = jnp.where(core == 0, *(cube_index(place_of, dims) for dims in LATE))
    base = core * 64 + 8 * jnp.where(core == 0, *(cube_index(place_of, dims) for dims in EARLY))
    mine = all_ref[pl.ds(block, 1), :]
    hit = iota((rows, LAB), 1) == base + aux_ref[:, 0:1].astype(jnp.int32)
    column = jnp.sum(jnp.where(hit, mine, 0.0), axis=1, keepdims=True)
    loss_ref[...] = as_row(column * aux_ref[:, 1:2], rows)
    bench, scored = labels_ref[0], labels_ref[1]
    kept = losses * scored
    ids = iota((BENCH, LAB), 0).astype(F32)
    sums, counts = jnp.zeros((BENCH, LAB), F32), jnp.zeros((BENCH, LAB), F32)
    for k in range(8):
        same = ids == bench[k : k + 1]
        sums += jnp.where(same, kept[k : k + 1], 0.0)
        counts += jnp.where(same, scored[k : k + 1], 0.0)
    sums = as_row(jnp.sum(sums, axis=1, keepdims=True), BENCH)
    counts = as_row(jnp.sum(counts, axis=1, keepdims=True), BENCH)
    mean_ref[...] = sums / jnp.maximum(counts, 1.0)
    count_ref[...] = counts


def final(parts, labels, aux):
    rows = aux.shape[0]
    outs = pl.pallas_call(
        final_kernel,
        out_shape=tuple(jax.ShapeDtypeStruct((1, n), F32) for n in (rows, BENCH, BENCH)),
        in_specs=[VMEM] * (len(parts) + 2),
        out_specs=(VMEM,) * 3,
        scratch_shapes=[pltpu.VMEM((8, LAB), F32)],
        compiler_params=pltpu.CompilerParams(vmem_limit_bytes=4 << 20),
        name="final",
    )(*parts, labels, aux)
    return tuple(v.reshape(-1) for v in outs)


def tied(*arrays):
    return lax.optimization_barrier(arrays)


def fetch_kernel(w_ref, out_ref, sem):
    move = pltpu.make_async_copy(w_ref, out_ref, sem)
    move.start()
    move.wait()


def fetch(w):
    return pl.pallas_call(
        fetch_kernel,
        out_shape=jax.ShapeDtypeStruct(w.shape, w.dtype),
        in_specs=[pl.BlockSpec(memory_space=pl.ANY)],
        out_specs=VMEM,
        scratch_shapes=[pltpu.SemaphoreType.DMA],
        compiler_params=pltpu.CompilerParams(vmem_limit_bytes=LIMIT),
        cost_estimate=pl.CostEstimate(flops=0, bytes_accessed=2 * w.size, transcendentals=0),
        name="fetch",
    )(w)


def body(hidden, head_weight, targets, bench_ids, valid, seq_lengths):
    x, aux = pack(hidden, targets, bench_ids, valid, seq_lengths)
    x = lax.all_to_all(x, "d", 0, 0, axis_index_groups=early_groups()).reshape(-1, x.shape[-1])
    near = [late_exchange(x, k) for k in range(3)]
    *near, w = tied(*near, fetch(head_weight.T))
    near_rows = [x, *near]
    own1 = score(w, near_rows)
    sib1 = score(w, [core_swap(jnp.concatenate(near_rows, 0))])
    far = [late_exchange(near[(k + 1) % 3], k) for k in range(3)]
    *far, own1, sib1 = tied(*far, own1, sib1)
    own2 = score(w, far)
    sib2 = score(w, [core_swap(jnp.concatenate(far, 0))])
    spans = zip(CUTS, CUTS[1:])
    last = jnp.concatenate(
        [late_exchange(far[(k + 1) % 3][i:j], k) for k, (i, j) in enumerate(spans)], 0
    )
    last, own2 = tied(last, own2)
    stats, labels = score_place(w, (own1, sib1, own2, sib2), [last, core_swap(last)])
    parts = [stats, core_swap(stats)]
    for axis in range(3):
        stats = jnp.stack(merged(parts))
        steps = [(axis, 0), (axis, 1)]
        parts = [stats, *(cross_exchange(stats, d) for d in (steps[:1], steps[1:], steps))]
    return final(parts, labels, aux)


def solution(mesh):
    flat = Mesh(mesh.devices.reshape(-1), ("d",))
    in_specs = (P("d", None), P(None, "d"), P("d"), P("d"), P("d"), P())
    return jax.shard_map(
        body, mesh=flat, in_specs=in_specs, out_specs=(P("d"), P(), P()), check_vma=False
    )
```

```python
import jax
import jax.numpy as jnp
from jax import lax
from jax.experimental import pallas as pl
from jax.experimental.pallas import tpu as pltpu
from jax.sharding import Mesh
from jax.sharding import PartitionSpec as P

BENCH = 40
N_DEV = 128
LAB = 128
CUTS = (0, 32, 64)
SETS = ((0, 1, 2, 4), (3, 6, 5), (7,))
F32 = jnp.float32
LIMIT = 12 << 20
BLOCK = 64
EARLY = (((2, 0), (1, 0), (0, 0)), ((2, 1), (1, 1), (0, 1)))
LATE = (EARLY[1], EARLY[0])


def coords(d):
    return (d // 32, (d // 4) % 4, d % 4), (d // 16) % 2


def cube_bits(p):
    return (p ^ (p >> 1)) & 1, p >> 1


def cube_index(place_of, dims):
    return sum(cube_bits(place_of[axis])[bit] << k for k, (axis, bit) in enumerate(dims))


def flipped(d, dims):
    p, core = coords(d)
    p = list(p)
    for axis, bit in dims:
        p[axis] = 3 - p[axis] if bit else p[axis] ^ 1
    return ((p[0] * 2 + core) * 4 + p[1]) * 4 + p[2]


def exchange(v, by_core):
    return lax.ppermute(v, "d", [(d, flipped(d, by_core[coords(d)[1]])) for d in range(N_DEV)])


def late_exchange(v, k):
    return exchange(v, [(dims[k % 3],) for dims in LATE])


def cross_exchange(v, dims):
    return lax.ppermute(v, "d", [(d, flipped(d, dims) ^ 16) for d in range(N_DEV)])


def early_groups():
    groups = {}
    for d in range(N_DEV):
        p, core = coords(d)
        groups.setdefault((core, cube_index(p, LATE[core])), []).append((cube_index(p, EARLY[core]), d))
    return [[d for _, d in sorted(group)] for group in groups.values()]


def core_swap(v):
    return lax.ppermute(v, "d", [(d, d ^ 16) for d in range(N_DEV)])


NT = (((1,), (1,)), ((), ()))
VMEM = pl.BlockSpec(memory_space=pltpu.VMEM)


def iota(shape, dim):
    return lax.broadcasted_iota(jnp.int32, shape, dim)


def as_column(row, n):
    eye = iota((n, n), 0) == iota((n, n), 1)
    return jnp.sum(jnp.where(eye, row, 0.0), axis=1, keepdims=True)


def as_row(column, n):
    eye = iota((n, n), 0) == iota((n, n), 1)
    return jnp.sum(jnp.where(eye, column, 0.0), axis=0, keepdims=True)


def running_sum(row, n):
    upto = jnp.where(iota((n, n), 0) <= iota((n, n), 1), 1.0, 0.0).astype(jnp.bfloat16)
    wide = jnp.broadcast_to(row, (8, n)).astype(jnp.bfloat16)
    return jnp.dot(wide, upto, preferred_element_type=F32)[0:1]


def pack_kernel(hidden_ref, ints_ref, x_ref, aux_ref):
    rows, depth = hidden_ref.shape
    kept = rows // 2
    ints = ints_ref[...]
    target, bench, valid = (ints[:, k * rows : (k + 1) * rows] for k in range(3))
    lengths = ints[:, 3 * rows :]
    seqs = lengths.shape[1]
    me = lax.axis_index("d")
    ends = running_sum(lengths.astype(F32), seqs).astype(jnp.int32) - 1
    position = me * rows + iota((rows, seqs), 0)
    is_end = jnp.max(jnp.where(ends == position, 1.0, 0.0), axis=1, keepdims=True)
    valid = valid.astype(F32)
    rank = running_sum(valid, rows) - 1.0
    token = iota((1, rows), 1).astype(F32)
    count = jnp.sum(valid, axis=1, keepdims=True)
    slot = jnp.where(valid > 0.5, rank, count + token - rank - 1.0)
    selector = jnp.where(iota((kept, rows), 0).astype(F32) == slot, 1.0, 0.0).astype(jnp.bfloat16)
    scored = as_column(valid, rows) * (1.0 - is_end)
    digits = [target >> 16, (target >> 8) & 255, target & 255, bench]
    lane = iota((rows, LAB), 1)
    labels = jnp.where(lane == 4, scored, 0.0)
    for k, digit in enumerate(digits):
        labels = jnp.where(lane == k, as_column(digit.astype(F32), rows), labels)
    picked = jnp.dot(selector, hidden_ref[...], preferred_element_type=F32).astype(jnp.bfloat16)
    tags = jnp.dot(selector, labels.astype(jnp.bfloat16), preferred_element_type=F32).astype(jnp.bfloat16)
    for k in range(x_ref.shape[0]):
        x_ref[k, :, :depth] = picked
        x_ref[k, :, depth:] = tags
    aux_ref[...] = jnp.where(lane == 0, as_column(slot, rows), jnp.where(lane == 1, scored, 0.0))


def pack(hidden, *ints):
    rows, depth = hidden.shape
    return pl.pallas_call(
        pack_kernel,
        out_shape=(
            jax.ShapeDtypeStruct((8, rows // 2, depth + LAB), jnp.bfloat16),
            jax.ShapeDtypeStruct((rows, LAB), F32),
        ),
        in_specs=[VMEM, VMEM],
        out_specs=(VMEM, VMEM),
        compiler_params=pltpu.CompilerParams(vmem_limit_bytes=4 << 20),
        name="pack",
    )(hidden, jnp.concatenate(ints).reshape(1, -1))


def scores(x_ref, w_ref, acc_ref):
    vocab, depth = w_ref.shape
    r, c = iota((8, LAB), 0), iota((8, LAB), 1)
    digit = jnp.where(c == 0, 65536.0, jnp.where(c == 1, 256.0, 1.0))
    sel = jnp.where((r == 5) & (c < 3), digit, jnp.where(((r == 3) | (r == 4)) & (r == c), 1.0, 0.0))
    labels = lax.dot_general(
        sel.astype(jnp.bfloat16), x_ref[:, depth:], NT, preferred_element_type=F32
    )
    acc_ref[...] = lax.dot_general(w_ref[...], x_ref[:, :depth], NT, preferred_element_type=F32)
    logits = acc_ref[...]
    top = jnp.max(logits, axis=0, keepdims=True)
    total = jnp.sum(jnp.exp(logits - top), axis=0, keepdims=True)
    local = labels[5:6].astype(jnp.int32) - lax.axis_index("d") * vocab
    target = jnp.sum(jnp.where(iota(logits.shape, 0) == local, logits, 0.0), axis=0, keepdims=True)
    k = iota((8, x_ref.shape[0]), 0)
    return jnp.where(k == 0, top, jnp.where(k == 1, total, jnp.where(k == 2, target, labels)))


def gather_rows(pieces, x_ref):
    at = 0
    for piece in pieces:
        x_ref[at : at + piece.shape[0], :] = piece[...]
        at += piece.shape[0]


def score_kernel(w_ref, *refs):
    *pieces, out_ref, x_ref, acc_ref = refs
    gather_rows(pieces, x_ref)
    out_ref[...] = scores(x_ref, w_ref, acc_ref)


def score(w, pieces):
    vocab, depth = w.shape
    rows = sum(p.shape[0] for p in pieces)
    return pl.pallas_call(
        score_kernel,
        out_shape=jax.ShapeDtypeStruct((8, rows), F32),
        in_specs=[VMEM] * (1 + len(pieces)),
        out_specs=VMEM,
        scratch_shapes=[
            pltpu.VMEM((rows, depth + LAB), jnp.bfloat16),
            pltpu.VMEM((vocab, rows), F32),
        ],
        compiler_params=pltpu.CompilerParams(vmem_limit_bytes=LIMIT),
        cost_estimate=pl.CostEstimate(
            flops=2 * rows * vocab * depth, bytes_accessed=2 * vocab * depth, transcendentals=rows * vocab
        ),
        name="score",
    )(w, *pieces)


def score_place_kernel(w_ref, *refs):
    *refs, stats_ref, labels_ref, x_ref, acc_ref, all_ref = refs
    done, pieces = refs[:4], refs[4:]
    gather_rows(pieces, x_ref)
    last = scores(x_ref, w_ref, acc_ref)
    place_of, core = coords(lax.axis_index("d"))
    blocks = [cube_index(place_of, LATE[k]) for k in range(2)]
    is_first = core == 0
    pairs = [(done[0][...], done[1][...]), (done[2][...], done[3][...]), (last[:, :BLOCK], last[:, BLOCK:])]
    for rels, (own, sib) in zip(SETS, pairs):
        by_core = (jnp.where(is_first, own, sib), jnp.where(is_first, sib, own))
        for i, rel in enumerate(rels):
            for side in range(2):
                to = side * BLOCK
                all_ref[blocks[side] ^ rel, :, to : to + BLOCK] = by_core[side][:, i * BLOCK : (i + 1) * BLOCK]
    for kind in range(3):
        stats_ref[kind] = all_ref[:, kind, :]
    for kind in range(2):
        labels_ref[kind] = all_ref[:, 3 + kind, :]


def score_place(w, done, pieces):
    vocab, depth = w.shape
    rows = sum(p.shape[0] for p in pieces)
    return pl.pallas_call(
        score_place_kernel,
        out_shape=(jax.ShapeDtypeStruct((3, 8, 128), F32), jax.ShapeDtypeStruct((2, 8, 128), F32)),
        in_specs=[VMEM] * (1 + len(done) + len(pieces)),
        out_specs=(VMEM, VMEM),
        scratch_shapes=[
            pltpu.VMEM((rows, depth + LAB), jnp.bfloat16),
            pltpu.VMEM((vocab, rows), F32),
            pltpu.VMEM((8, 8, 128), F32),
        ],
        compiler_params=pltpu.CompilerParams(vmem_limit_bytes=LIMIT),
        cost_estimate=pl.CostEstimate(
            flops=2 * rows * vocab * depth, bytes_accessed=2 * vocab * depth, transcendentals=rows * vocab
        ),
        name="score_place",
    )(w, *done, *pieces)


def merged(parts):
    best = parts[0][0]
    for p in parts[1:]:
        best = jnp.maximum(best, p[0])
    total = sum(p[1] * jnp.exp(p[0] - best) for p in parts)
    return best, total, sum(p[2] for p in parts)


def final_kernel(*refs):
    *parts, labels_ref, aux_ref, loss_ref, mean_ref, count_ref, all_ref = refs
    best, total, target = merged(parts)
    losses = best + jnp.log(total) - target
    all_ref[...] = losses
    rows = aux_ref.shape[0]
    place_of, core = coords(lax.axis_index("d"))
    block = jnp.where(core == 0, *(cube_index(place_of, dims) for dims in LATE))
    base = core * 64 + 8 * jnp.where(core == 0, *(cube_index(place_of, dims) for dims in EARLY))
    mine = all_ref[pl.ds(block, 1), :]
    hit = iota((rows, LAB), 1) == base + aux_ref[:, 0:1].astype(jnp.int32)
    column = jnp.sum(jnp.where(hit, mine, 0.0), axis=1, keepdims=True)
    loss_ref[...] = as_row(column * aux_ref[:, 1:2], rows)
    bench, scored = labels_ref[0], labels_ref[1]
    kept = losses * scored
    ids = iota((BENCH, LAB), 0).astype(F32)
    sums, counts = jnp.zeros((BENCH, LAB), F32), jnp.zeros((BENCH, LAB), F32)
    for k in range(8):
        same = ids == bench[k : k + 1]
        sums += jnp.where(same, kept[k : k + 1], 0.0)
        counts += jnp.where(same, scored[k : k + 1], 0.0)
    sums = as_row(jnp.sum(sums, axis=1, keepdims=True), BENCH)
    counts = as_row(jnp.sum(counts, axis=1, keepdims=True), BENCH)
    mean_ref[...] = sums / jnp.maximum(counts, 1.0)
    count_ref[...] = counts


def final(parts, labels, aux):
    rows = aux.shape[0]
    outs = pl.pallas_call(
        final_kernel,
        out_shape=tuple(jax.ShapeDtypeStruct((1, n), F32) for n in (rows, BENCH, BENCH)),
        in_specs=[VMEM] * (len(parts) + 2),
        out_specs=(VMEM,) * 3,
        scratch_shapes=[pltpu.VMEM((8, LAB), F32)],
        compiler_params=pltpu.CompilerParams(vmem_limit_bytes=4 << 20),
        name="final",
    )(*parts, labels, aux)
    return tuple(v.reshape(-1) for v in outs)


def tied(*arrays):
    return lax.optimization_barrier(arrays)


def fetch_kernel(w_ref, out_ref, sem):
    move = pltpu.make_async_copy(w_ref, out_ref, sem)
    move.start()
    move.wait()


def fetch(w):
    return pl.pallas_call(
        fetch_kernel,
        out_shape=jax.ShapeDtypeStruct(w.shape, w.dtype),
        in_specs=[pl.BlockSpec(memory_space=pl.ANY)],
        out_specs=VMEM,
        scratch_shapes=[pltpu.SemaphoreType.DMA],
        compiler_params=pltpu.CompilerParams(vmem_limit_bytes=LIMIT),
        cost_estimate=pl.CostEstimate(flops=0, bytes_accessed=2 * w.size, transcendentals=0),
        name="fetch",
    )(w)


def body(hidden, head_weight, targets, bench_ids, valid, seq_lengths):
    x, aux = pack(hidden, targets, bench_ids, valid, seq_lengths)
    x = lax.all_to_all(x, "d", 0, 0, axis_index_groups=early_groups()).reshape(-1, x.shape[-1])
    near = [late_exchange(x, k) for k in range(3)]
    near[0], w = tied(near[0], fetch(head_weight.T))
    near_rows = [x, *near]
    own1 = score(w, near_rows)
    sib1 = score(w, [core_swap(jnp.concatenate(near_rows, 0))])
    far = [late_exchange(near[(k + 1) % 3], k) for k in range(3)]
    *far, own1, sib1 = tied(*far, own1, sib1)
    own2 = score(w, far)
    sib2 = score(w, [core_swap(jnp.concatenate(far, 0))])
    spans = zip(CUTS, CUTS[1:])
    last = jnp.concatenate(
        [late_exchange(far[(k + 1) % 3][i:j], k) for k, (i, j) in enumerate(spans)], 0
    )
    last, own2 = tied(last, own2)
    stats, labels = score_place(w, (own1, sib1, own2, sib2), [last, core_swap(last)])
    parts = [stats, core_swap(stats)]
    for axis in range(3):
        stats = jnp.stack(merged(parts))
        steps = [(axis, 0), (axis, 1)]
        parts = [stats, *(cross_exchange(stats, d) for d in (steps[:1], steps[1:], steps))]
    return final(parts, labels, aux)


def solution(mesh):
    flat = Mesh(mesh.devices.reshape(-1), ("d",))
    in_specs = (P("d", None), P(None, "d"), P("d"), P("d"), P("d"), P())
    return jax.shard_map(
        body, mesh=flat, in_specs=in_specs, out_specs=(P("d"), P(), P()), check_vma=False
    )
```

```python
import jax
import jax.numpy as jnp
from jax import lax
from jax.experimental import pallas as pl
from jax.experimental.pallas import tpu as pltpu
from jax.sharding import Mesh
from jax.sharding import PartitionSpec as P

BENCH = 40
N_DEV = 128
LAB = 128
CUTS = (0, 24, 48, 64)
SETS = ((0, 1, 2, 4), (3, 6, 5), (7,))
F32 = jnp.float32
LIMIT = 12 << 20
BLOCK = 64
EARLY = (((2, 0), (1, 0), (0, 0)), ((2, 1), (1, 1), (0, 1)))
LATE = (EARLY[1], EARLY[0])


def coords(d):
    return (d // 32, (d // 4) % 4, d % 4), (d // 16) % 2


def cube_bits(p):
    return (p ^ (p >> 1)) & 1, p >> 1


def cube_index(place_of, dims):
    return sum(cube_bits(place_of[axis])[bit] << k for k, (axis, bit) in enumerate(dims))


def flipped(d, dims):
    p, core = coords(d)
    p = list(p)
    for axis, bit in dims:
        p[axis] = 3 - p[axis] if bit else p[axis] ^ 1
    return ((p[0] * 2 + core) * 4 + p[1]) * 4 + p[2]


def exchange(v, by_core):
    return lax.ppermute(v, "d", [(d, flipped(d, by_core[coords(d)[1]])) for d in range(N_DEV)])


def late_exchange(v, k):
    return exchange(v, [(dims[k % 3],) for dims in LATE])


def cross_exchange(v, dims):
    return lax.ppermute(v, "d", [(d, flipped(d, dims) ^ 16) for d in range(N_DEV)])


def early_groups():
    groups = {}
    for d in range(N_DEV):
        p, core = coords(d)
        groups.setdefault((core, cube_index(p, LATE[core])), []).append((cube_index(p, EARLY[core]), d))
    return [[d for _, d in sorted(group)] for group in groups.values()]


def core_swap(v):
    return lax.ppermute(v, "d", [(d, d ^ 16) for d in range(N_DEV)])


NT = (((1,), (1,)), ((), ()))
VMEM = pl.BlockSpec(memory_space=pltpu.VMEM)


def iota(shape, dim):
    return lax.broadcasted_iota(jnp.int32, shape, dim)


def as_column(row, n):
    eye = iota((n, n), 0) == iota((n, n), 1)
    return jnp.sum(jnp.where(eye, row, 0.0), axis=1, keepdims=True)


def as_row(column, n):
    eye = iota((n, n), 0) == iota((n, n), 1)
    return jnp.sum(jnp.where(eye, column, 0.0), axis=0, keepdims=True)


def running_sum(row, n):
    upto = jnp.where(iota((n, n), 0) <= iota((n, n), 1), 1.0, 0.0).astype(jnp.bfloat16)
    wide = jnp.broadcast_to(row, (8, n)).astype(jnp.bfloat16)
    return jnp.dot(wide, upto, preferred_element_type=F32)[0:1]


def pack_kernel(hidden_ref, ints_ref, x_ref, aux_ref):
    rows, depth = hidden_ref.shape
    kept = rows // 2
    ints = ints_ref[...]
    target, bench, valid = (ints[:, k * rows : (k + 1) * rows] for k in range(3))
    lengths = ints[:, 3 * rows :]
    seqs = lengths.shape[1]
    me = lax.axis_index("d")
    ends = running_sum(lengths.astype(F32), seqs).astype(jnp.int32) - 1
    position = me * rows + iota((rows, seqs), 0)
    is_end = jnp.max(jnp.where(ends == position, 1.0, 0.0), axis=1, keepdims=True)
    valid = valid.astype(F32)
    rank = running_sum(valid, rows) - 1.0
    token = iota((1, rows), 1).astype(F32)
    count = jnp.sum(valid, axis=1, keepdims=True)
    slot = jnp.where(valid > 0.5, rank, count + token - rank - 1.0)
    selector = jnp.where(iota((kept, rows), 0).astype(F32) == slot, 1.0, 0.0).astype(jnp.bfloat16)
    scored = as_column(valid, rows) * (1.0 - is_end)
    digits = [target >> 16, (target >> 8) & 255, target & 255, bench]
    lane = iota((rows, LAB), 1)
    labels = jnp.where(lane == 4, scored, 0.0)
    for k, digit in enumerate(digits):
        labels = jnp.where(lane == k, as_column(digit.astype(F32), rows), labels)
    picked = jnp.dot(selector, hidden_ref[...], preferred_element_type=F32).astype(jnp.bfloat16)
    tags = jnp.dot(selector, labels.astype(jnp.bfloat16), preferred_element_type=F32).astype(jnp.bfloat16)
    for k in range(x_ref.shape[0]):
        x_ref[k, :, :depth] = picked
        x_ref[k, :, depth:] = tags
    aux_ref[...] = jnp.where(lane == 0, as_column(slot, rows), jnp.where(lane == 1, scored, 0.0))


def pack(hidden, *ints):
    rows, depth = hidden.shape
    return pl.pallas_call(
        pack_kernel,
        out_shape=(
            jax.ShapeDtypeStruct((8, rows // 2, depth + LAB), jnp.bfloat16),
            jax.ShapeDtypeStruct((rows, LAB), F32),
        ),
        in_specs=[VMEM, VMEM],
        out_specs=(VMEM, VMEM),
        compiler_params=pltpu.CompilerParams(vmem_limit_bytes=4 << 20),
        name="pack",
    )(hidden, jnp.concatenate(ints).reshape(1, -1))


def scores(x_ref, w_ref, acc_ref):
    vocab, depth = w_ref.shape
    r, c = iota((8, LAB), 0), iota((8, LAB), 1)
    digit = jnp.where(c == 0, 65536.0, jnp.where(c == 1, 256.0, 1.0))
    sel = jnp.where((r == 5) & (c < 3), digit, jnp.where(((r == 3) | (r == 4)) & (r == c), 1.0, 0.0))
    labels = lax.dot_general(
        sel.astype(jnp.bfloat16), x_ref[:, depth:], NT, preferred_element_type=F32
    )
    acc_ref[...] = lax.dot_general(w_ref[...], x_ref[:, :depth], NT, preferred_element_type=F32)
    logits = acc_ref[...]
    top = jnp.max(logits, axis=0, keepdims=True)
    total = jnp.sum(jnp.exp(logits - top), axis=0, keepdims=True)
    local = labels[5:6].astype(jnp.int32) - lax.axis_index("d") * vocab
    target = jnp.sum(jnp.where(iota(logits.shape, 0) == local, logits, 0.0), axis=0, keepdims=True)
    k = iota((8, x_ref.shape[0]), 0)
    return jnp.where(k == 0, top, jnp.where(k == 1, total, jnp.where(k == 2, target, labels)))


def gather_rows(pieces, x_ref):
    at = 0
    for piece in pieces:
        x_ref[at : at + piece.shape[0], :] = piece[...]
        at += piece.shape[0]


def score_kernel(w_ref, *refs):
    *pieces, out_ref, x_ref, acc_ref = refs
    gather_rows(pieces, x_ref)
    out_ref[...] = scores(x_ref, w_ref, acc_ref)


def score(w, pieces):
    vocab, depth = w.shape
    rows = sum(p.shape[0] for p in pieces)
    return pl.pallas_call(
        score_kernel,
        out_shape=jax.ShapeDtypeStruct((8, rows), F32),
        in_specs=[VMEM] * (1 + len(pieces)),
        out_specs=VMEM,
        scratch_shapes=[
            pltpu.VMEM((rows, depth + LAB), jnp.bfloat16),
            pltpu.VMEM((vocab, rows), F32),
        ],
        compiler_params=pltpu.CompilerParams(vmem_limit_bytes=LIMIT),
        cost_estimate=pl.CostEstimate(
            flops=2 * rows * vocab * depth, bytes_accessed=2 * vocab * depth, transcendentals=rows * vocab
        ),
        name="score",
    )(w, *pieces)


def score_place_kernel(w_ref, *refs):
    *refs, stats_ref, labels_ref, x_ref, acc_ref, all_ref = refs
    done, pieces = refs[:4], refs[4:]
    gather_rows(pieces, x_ref)
    last = scores(x_ref, w_ref, acc_ref)
    place_of, core = coords(lax.axis_index("d"))
    blocks = [cube_index(place_of, LATE[k]) for k in range(2)]
    is_first = core == 0
    pairs = [(done[0][...], done[1][...]), (done[2][...], done[3][...]), (last[:, :BLOCK], last[:, BLOCK:])]
    for rels, (own, sib) in zip(SETS, pairs):
        by_core = (jnp.where(is_first, own, sib), jnp.where(is_first, sib, own))
        for i, rel in enumerate(rels):
            for side in range(2):
                to = side * BLOCK
                all_ref[blocks[side] ^ rel, :, to : to + BLOCK] = by_core[side][:, i * BLOCK : (i + 1) * BLOCK]
    for kind in range(3):
        stats_ref[kind] = all_ref[:, kind, :]
    for kind in range(2):
        labels_ref[kind] = all_ref[:, 3 + kind, :]


def score_place(w, done, pieces):
    vocab, depth = w.shape
    rows = sum(p.shape[0] for p in pieces)
    return pl.pallas_call(
        score_place_kernel,
        out_shape=(jax.ShapeDtypeStruct((3, 8, 128), F32), jax.ShapeDtypeStruct((2, 8, 128), F32)),
        in_specs=[VMEM] * (1 + len(done) + len(pieces)),
        out_specs=(VMEM, VMEM),
        scratch_shapes=[
            pltpu.VMEM((rows, depth + LAB), jnp.bfloat16),
            pltpu.VMEM((vocab, rows), F32),
            pltpu.VMEM((8, 8, 128), F32),
        ],
        compiler_params=pltpu.CompilerParams(vmem_limit_bytes=LIMIT),
        cost_estimate=pl.CostEstimate(
            flops=2 * rows * vocab * depth, bytes_accessed=2 * vocab * depth, transcendentals=rows * vocab
        ),
        name="score_place",
    )(w, *done, *pieces)


def merged(parts):
    best = parts[0][0]
    for p in parts[1:]:
        best = jnp.maximum(best, p[0])
    total = sum(p[1] * jnp.exp(p[0] - best) for p in parts)
    return best, total, sum(p[2] for p in parts)


def final_kernel(*refs):
    *parts, labels_ref, aux_ref, loss_ref, mean_ref, count_ref, all_ref = refs
    best, total, target = merged(parts)
    losses = best + jnp.log(total) - target
    all_ref[...] = losses
    rows = aux_ref.shape[0]
    place_of, core = coords(lax.axis_index("d"))
    block = jnp.where(core == 0, *(cube_index(place_of, dims) for dims in LATE))
    base = core * 64 + 8 * jnp.where(core == 0, *(cube_index(place_of, dims) for dims in EARLY))
    mine = all_ref[pl.ds(block, 1), :]
    hit = iota((rows, LAB), 1) == base + aux_ref[:, 0:1].astype(jnp.int32)
    column = jnp.sum(jnp.where(hit, mine, 0.0), axis=1, keepdims=True)
    loss_ref[...] = as_row(column * aux_ref[:, 1:2], rows)
    bench, scored = labels_ref[0], labels_ref[1]
    kept = losses * scored
    ids = iota((BENCH, LAB), 0).astype(F32)
    sums, counts = jnp.zeros((BENCH, LAB), F32), jnp.zeros((BENCH, LAB), F32)
    for k in range(8):
        same = ids == bench[k : k + 1]
        sums += jnp.where(same, kept[k : k + 1], 0.0)
        counts += jnp.where(same, scored[k : k + 1], 0.0)
    sums = as_row(jnp.sum(sums, axis=1, keepdims=True), BENCH)
    counts = as_row(jnp.sum(counts, axis=1, keepdims=True), BENCH)
    mean_ref[...] = sums / jnp.maximum(counts, 1.0)
    count_ref[...] = counts


def final(parts, labels, aux):
    rows = aux.shape[0]
    outs = pl.pallas_call(
        final_kernel,
        out_shape=tuple(jax.ShapeDtypeStruct((1, n), F32) for n in (rows, BENCH, BENCH)),
        in_specs=[VMEM] * (len(parts) + 2),
        out_specs=(VMEM,) * 3,
        scratch_shapes=[pltpu.VMEM((8, LAB), F32)],
        compiler_params=pltpu.CompilerParams(vmem_limit_bytes=4 << 20),
        name="final",
    )(*parts, labels, aux)
    return tuple(v.reshape(-1) for v in outs)


def tied(*arrays):
    return lax.optimization_barrier(arrays)


def fetch_kernel(w_ref, out_ref, sem):
    move = pltpu.make_async_copy(w_ref, out_ref, sem)
    move.start()
    move.wait()


def fetch(w):
    return pl.pallas_call(
        fetch_kernel,
        out_shape=jax.ShapeDtypeStruct(w.shape, w.dtype),
        in_specs=[pl.BlockSpec(memory_space=pl.ANY)],
        out_specs=VMEM,
        scratch_shapes=[pltpu.SemaphoreType.DMA],
        compiler_params=pltpu.CompilerParams(vmem_limit_bytes=LIMIT),
        cost_estimate=pl.CostEstimate(flops=0, bytes_accessed=2 * w.size, transcendentals=0),
        name="fetch",
    )(w)


def body(hidden, head_weight, targets, bench_ids, valid, seq_lengths):
    x, aux = pack(hidden, targets, bench_ids, valid, seq_lengths)
    x = lax.all_to_all(x, "d", 0, 0, axis_index_groups=early_groups()).reshape(-1, x.shape[-1])
    near = [late_exchange(x, k) for k in range(3)]
    near[0], w = tied(near[0], fetch(head_weight.T))
    near_rows = [x, *near]
    own1 = score(w, near_rows)
    sib1 = score(w, [core_swap(jnp.concatenate(near_rows, 0))])
    far = [late_exchange(near[(k + 1) % 3], k) for k in range(3)]
    *far, own1, sib1 = tied(*far, own1, sib1)
    own2 = score(w, far)
    sib2 = score(w, [core_swap(jnp.concatenate(far, 0))])
    spans = zip(CUTS, CUTS[1:])
    last = jnp.concatenate(
        [late_exchange(far[(k + 1) % 3][i:j], k) for k, (i, j) in enumerate(spans)], 0
    )
    last, own2 = tied(last, own2)
    stats, labels = score_place(w, (own1, sib1, own2, sib2), [last, core_swap(last)])
    parts = [stats, core_swap(stats)]
    for axis in range(3):
        stats = jnp.stack(merged(parts))
        steps = [(axis, 0), (axis, 1)]
        parts = [stats, *(cross_exchange(stats, d) for d in (steps[:1], steps[1:], steps))]
    return final(parts, labels, aux)


def solution(mesh):
    flat = Mesh(mesh.devices.reshape(-1), ("d",))
    in_specs = (P("d", None), P(None, "d"), P("d"), P("d"), P("d"), P())
    return jax.shard_map(
        body, mesh=flat, in_specs=in_specs, out_specs=(P("d"), P(), P()), check_vma=False
    )
```

```python
import jax
import jax.numpy as jnp
from jax import lax
from jax.experimental import pallas as pl
from jax.experimental.pallas import tpu as pltpu
from jax.sharding import Mesh
from jax.sharding import PartitionSpec as P

BENCH = 40
N_DEV = 128
LAB = 128
CUTS = (0, 32, 64)
SETS = ((0, 1, 2, 4), (3, 6, 5), (7,))
F32 = jnp.float32
LIMIT = 12 << 20
BLOCK = 64
EARLY = (((2, 0), (1, 0), (0, 0)), ((2, 1), (1, 1), (0, 1)))
LATE = (EARLY[1], EARLY[0])


def coords(d):
    return (d // 32, (d // 4) % 4, d % 4), (d // 16) % 2


def cube_bits(p):
    return (p ^ (p >> 1)) & 1, p >> 1


def cube_index(place_of, dims):
    return sum(cube_bits(place_of[axis])[bit] << k for k, (axis, bit) in enumerate(dims))


def flipped(d, dims):
    p, core = coords(d)
    p = list(p)
    for axis, bit in dims:
        p[axis] = 3 - p[axis] if bit else p[axis] ^ 1
    return ((p[0] * 2 + core) * 4 + p[1]) * 4 + p[2]


def exchange(v, by_core):
    return lax.ppermute(v, "d", [(d, flipped(d, by_core[coords(d)[1]])) for d in range(N_DEV)])


def late_exchange(v, k):
    return exchange(v, [(dims[k % 3],) for dims in LATE])


def cross_exchange(v, dims):
    return lax.ppermute(v, "d", [(d, flipped(d, dims) ^ 16) for d in range(N_DEV)])


def early_groups():
    groups = {}
    for d in range(N_DEV):
        p, core = coords(d)
        groups.setdefault((core, cube_index(p, LATE[core])), []).append((cube_index(p, EARLY[core]), d))
    return [[d for _, d in sorted(group)] for group in groups.values()]


def core_swap(v):
    return lax.ppermute(v, "d", [(d, d ^ 16) for d in range(N_DEV)])


NT = (((1,), (1,)), ((), ()))
VMEM = pl.BlockSpec(memory_space=pltpu.VMEM)


def iota(shape, dim):
    return lax.broadcasted_iota(jnp.int32, shape, dim)


def as_column(row, n):
    eye = iota((n, n), 0) == iota((n, n), 1)
    return jnp.sum(jnp.where(eye, row, 0.0), axis=1, keepdims=True)


def as_row(column, n):
    eye = iota((n, n), 0) == iota((n, n), 1)
    return jnp.sum(jnp.where(eye, column, 0.0), axis=0, keepdims=True)


def running_sum(row, n):
    upto = jnp.where(iota((n, n), 0) <= iota((n, n), 1), 1.0, 0.0).astype(jnp.bfloat16)
    wide = jnp.broadcast_to(row, (8, n)).astype(jnp.bfloat16)
    return jnp.dot(wide, upto, preferred_element_type=F32)[0:1]


def pack_kernel(hidden_ref, ints_ref, x_ref, aux_ref):
    rows, depth = hidden_ref.shape
    kept = rows // 2
    ints = ints_ref[...]
    target, bench, valid = (ints[:, k * rows : (k + 1) * rows] for k in range(3))
    lengths = ints[:, 3 * rows :]
    seqs = lengths.shape[1]
    me = lax.axis_index("d")
    ends = running_sum(lengths.astype(F32), seqs).astype(jnp.int32) - 1
    position = me * rows + iota((rows, seqs), 0)
    is_end = jnp.max(jnp.where(ends == position, 1.0, 0.0), axis=1, keepdims=True)
    valid = valid.astype(F32)
    rank = running_sum(valid, rows) - 1.0
    token = iota((1, rows), 1).astype(F32)
    count = jnp.sum(valid, axis=1, keepdims=True)
    slot = jnp.where(valid > 0.5, rank, count + token - rank - 1.0)
    selector = jnp.where(iota((kept, rows), 0).astype(F32) == slot, 1.0, 0.0).astype(jnp.bfloat16)
    scored = as_column(valid, rows) * (1.0 - is_end)
    digits = [target >> 16, (target >> 8) & 255, target & 255, bench]
    lane = iota((rows, LAB), 1)
    labels = jnp.where(lane == 4, scored, 0.0)
    for k, digit in enumerate(digits):
        labels = jnp.where(lane == k, as_column(digit.astype(F32), rows), labels)
    picked = jnp.dot(selector, hidden_ref[...], preferred_element_type=F32).astype(jnp.bfloat16)
    tags = jnp.dot(selector, labels.astype(jnp.bfloat16), preferred_element_type=F32).astype(jnp.bfloat16)
    for k in range(x_ref.shape[0]):
        x_ref[k, :, :depth] = picked
        x_ref[k, :, depth:] = tags
    aux_ref[...] = jnp.where(lane == 0, as_column(slot, rows), jnp.where(lane == 1, scored, 0.0))


def pack(hidden, *ints):
    rows, depth = hidden.shape
    return pl.pallas_call(
        pack_kernel,
        out_shape=(
            jax.ShapeDtypeStruct((8, rows // 2, depth + LAB), jnp.bfloat16),
            jax.ShapeDtypeStruct((rows, LAB), F32),
        ),
        in_specs=[VMEM, VMEM],
        out_specs=(VMEM, VMEM),
        compiler_params=pltpu.CompilerParams(vmem_limit_bytes=4 << 20),
        name="pack",
    )(hidden, jnp.concatenate(ints).reshape(1, -1))


def scores(x_ref, w_ref, acc_ref):
    vocab, depth = w_ref.shape
    r, c = iota((8, LAB), 0), iota((8, LAB), 1)
    digit = jnp.where(c == 0, 65536.0, jnp.where(c == 1, 256.0, 1.0))
    sel = jnp.where((r == 5) & (c < 3), digit, jnp.where(((r == 3) | (r == 4)) & (r == c), 1.0, 0.0))
    labels = lax.dot_general(
        sel.astype(jnp.bfloat16), x_ref[:, depth:], NT, preferred_element_type=F32
    )
    acc_ref[...] = lax.dot_general(w_ref[...], x_ref[:, :depth], NT, preferred_element_type=F32)
    logits = acc_ref[...]
    top = jnp.max(logits, axis=0, keepdims=True)
    total = jnp.sum(jnp.exp(logits - top), axis=0, keepdims=True)
    local = labels[5:6].astype(jnp.int32) - lax.axis_index("d") * vocab
    target = jnp.sum(jnp.where(iota(logits.shape, 0) == local, logits, 0.0), axis=0, keepdims=True)
    k = iota((8, x_ref.shape[0]), 0)
    return jnp.where(k == 0, top, jnp.where(k == 1, total, jnp.where(k == 2, target, labels)))


def gather_rows(pieces, x_ref):
    at = 0
    for piece in pieces:
        x_ref[at : at + piece.shape[0], :] = piece[...]
        at += piece.shape[0]


def score_kernel(w_ref, *refs):
    *pieces, out_ref, x_ref, acc_ref = refs
    gather_rows(pieces, x_ref)
    out_ref[...] = scores(x_ref, w_ref, acc_ref)


def score(w, pieces):
    vocab, depth = w.shape
    rows = sum(p.shape[0] for p in pieces)
    return pl.pallas_call(
        score_kernel,
        out_shape=jax.ShapeDtypeStruct((8, rows), F32),
        in_specs=[VMEM] * (1 + len(pieces)),
        out_specs=VMEM,
        scratch_shapes=[
            pltpu.VMEM((rows, depth + LAB), jnp.bfloat16),
            pltpu.VMEM((vocab, rows), F32),
        ],
        compiler_params=pltpu.CompilerParams(vmem_limit_bytes=LIMIT),
        cost_estimate=pl.CostEstimate(
            flops=2 * rows * vocab * depth, bytes_accessed=2 * vocab * depth, transcendentals=rows * vocab
        ),
        name="score",
    )(w, *pieces)


def score_place_kernel(w_ref, *refs):
    *refs, stats_ref, labels_ref, x_ref, acc_ref, all_ref = refs
    done, pieces = refs[:4], refs[4:]
    gather_rows(pieces, x_ref)
    last = scores(x_ref, w_ref, acc_ref)
    place_of, core = coords(lax.axis_index("d"))
    blocks = [cube_index(place_of, LATE[k]) for k in range(2)]
    is_first = core == 0
    pairs = [(done[0][...], done[1][...]), (done[2][...], done[3][...]), (last[:, :BLOCK], last[:, BLOCK:])]
    for rels, (own, sib) in zip(SETS, pairs):
        by_core = (jnp.where(is_first, own, sib), jnp.where(is_first, sib, own))
        for i, rel in enumerate(rels):
            for side in range(2):
                to = side * BLOCK
                all_ref[blocks[side] ^ rel, :, to : to + BLOCK] = by_core[side][:, i * BLOCK : (i + 1) * BLOCK]
    for kind in range(3):
        stats_ref[kind] = all_ref[:, kind, :]
    for kind in range(2):
        labels_ref[kind] = all_ref[:, 3 + kind, :]


def score_place(w, done, pieces):
    vocab, depth = w.shape
    rows = sum(p.shape[0] for p in pieces)
    return pl.pallas_call(
        score_place_kernel,
        out_shape=(jax.ShapeDtypeStruct((3, 8, 128), F32), jax.ShapeDtypeStruct((2, 8, 128), F32)),
        in_specs=[VMEM] * (1 + len(done) + len(pieces)),
        out_specs=(VMEM, VMEM),
        scratch_shapes=[
            pltpu.VMEM((rows, depth + LAB), jnp.bfloat16),
            pltpu.VMEM((vocab, rows), F32),
            pltpu.VMEM((8, 8, 128), F32),
        ],
        compiler_params=pltpu.CompilerParams(vmem_limit_bytes=LIMIT),
        cost_estimate=pl.CostEstimate(
            flops=2 * rows * vocab * depth, bytes_accessed=2 * vocab * depth, transcendentals=rows * vocab
        ),
        name="score_place",
    )(w, *done, *pieces)


def merged(parts):
    best = parts[0][0]
    for p in parts[1:]:
        best = jnp.maximum(best, p[0])
    total = sum(p[1] * jnp.exp(p[0] - best) for p in parts)
    return best, total, sum(p[2] for p in parts)


def final_kernel(*refs):
    *parts, labels_ref, aux_ref, loss_ref, mean_ref, count_ref, all_ref = refs
    best, total, target = merged(parts)
    losses = best + jnp.log(total) - target
    all_ref[...] = losses
    rows = aux_ref.shape[0]
    place_of, core = coords(lax.axis_index("d"))
    block = jnp.where(core == 0, *(cube_index(place_of, dims) for dims in LATE))
    base = core * 64 + 8 * jnp.where(core == 0, *(cube_index(place_of, dims) for dims in EARLY))
    mine = all_ref[pl.ds(block, 1), :]
    hit = iota((rows, LAB), 1) == base + aux_ref[:, 0:1].astype(jnp.int32)
    column = jnp.sum(jnp.where(hit, mine, 0.0), axis=1, keepdims=True)
    loss_ref[...] = as_row(column * aux_ref[:, 1:2], rows)
    bench, scored = labels_ref[0], labels_ref[1]
    kept = losses * scored
    ids = iota((BENCH, LAB), 0).astype(F32)
    sums, counts = jnp.zeros((BENCH, LAB), F32), jnp.zeros((BENCH, LAB), F32)
    for k in range(8):
        same = ids == bench[k : k + 1]
        sums += jnp.where(same, kept[k : k + 1], 0.0)
        counts += jnp.where(same, scored[k : k + 1], 0.0)
    sums = as_row(jnp.sum(sums, axis=1, keepdims=True), BENCH)
    counts = as_row(jnp.sum(counts, axis=1, keepdims=True), BENCH)
    mean_ref[...] = sums / jnp.maximum(counts, 1.0)
    count_ref[...] = counts


def final(parts, labels, aux):
    rows = aux.shape[0]
    outs = pl.pallas_call(
        final_kernel,
        out_shape=tuple(jax.ShapeDtypeStruct((1, n), F32) for n in (rows, BENCH, BENCH)),
        in_specs=[VMEM] * (len(parts) + 2),
        out_specs=(VMEM,) * 3,
        scratch_shapes=[pltpu.VMEM((8, LAB), F32)],
        compiler_params=pltpu.CompilerParams(vmem_limit_bytes=4 << 20),
        name="final",
    )(*parts, labels, aux)
    return tuple(v.reshape(-1) for v in outs)


def tied(*arrays):
    return lax.optimization_barrier(arrays)


def fetch_kernel(w_ref, out_ref, sem):
    move = pltpu.make_async_copy(w_ref, out_ref, sem)
    move.start()
    move.wait()


def fetch(w):
    return pl.pallas_call(
        fetch_kernel,
        out_shape=jax.ShapeDtypeStruct(w.shape, w.dtype),
        in_specs=[pl.BlockSpec(memory_space=pl.ANY)],
        out_specs=VMEM,
        scratch_shapes=[pltpu.SemaphoreType.DMA],
        compiler_params=pltpu.CompilerParams(vmem_limit_bytes=LIMIT),
        cost_estimate=pl.CostEstimate(flops=0, bytes_accessed=2 * w.size, transcendentals=0),
        name="fetch",
    )(w)


def body(hidden, head_weight, targets, bench_ids, valid, seq_lengths):
    x, aux = pack(hidden, targets, bench_ids, valid, seq_lengths)
    x = lax.all_to_all(x, "d", 0, 0, axis_index_groups=early_groups()).reshape(-1, x.shape[-1])
    near = [late_exchange(x, k) for k in range(3)]
    near[1], w = tied(near[1], fetch(head_weight.T))
    near_rows = [x, *near]
    own1 = score(w, near_rows)
    sib1 = score(w, [core_swap(jnp.concatenate(near_rows, 0))])
    far = [late_exchange(near[(k + 1) % 3], k) for k in range(3)]
    *far, own1, sib1 = tied(*far, own1, sib1)
    own2 = score(w, far)
    sib2 = score(w, [core_swap(jnp.concatenate(far, 0))])
    spans = zip(CUTS, CUTS[1:])
    last = jnp.concatenate(
        [late_exchange(far[(k + 1) % 3][i:j], k) for k, (i, j) in enumerate(spans)], 0
    )
    last, own2 = tied(last, own2)
    stats, labels = score_place(w, (own1, sib1, own2, sib2), [last, core_swap(last)])
    parts = [stats, core_swap(stats)]
    for axis in range(3):
        stats = jnp.stack(merged(parts))
        steps = [(axis, 0), (axis, 1)]
        parts = [stats, *(cross_exchange(stats, d) for d in (steps[:1], steps[1:], steps))]
    return final(parts, labels, aux)


def solution(mesh):
    flat = Mesh(mesh.devices.reshape(-1), ("d",))
    in_specs = (P("d", None), P(None, "d"), P("d"), P("d"), P("d"), P())
    return jax.shard_map(
        body, mesh=flat, in_specs=in_specs, out_specs=(P("d"), P(), P()), check_vma=False
    )
```
